768 devices in a mesh: grp: 16 (over y, core), shard: 48 (over x, z).
Axes of the slice: x: 4, y: 8, z: 12, core: 2. Of those that a mesh axis runs over, the one named last changes fastest.
Arguments:
- points: bfloat16 [786432, 768], P(('grp', 'shard'))
- serve_new: int32 [36864, 16], P(('grp', 'shard')), may hold values from 0 to 1023
- serve_old: int32 [12288, 32], P(('grp', 'shard')), may hold values from 0 to 1023
- count_new: int32 [36864, 1], P(('grp', 'shard')), may hold values from 0 to 16, as said below
- count_old: int32 [12288, 1], P(('grp', 'shard')), may hold values from 0 to 32, as said below
Outputs:
- nearest: float32 [786432, 16], P(('grp', 'shard'))
- reverse: float32 [786432], P(('grp', 'shard'))
The draws below stay inside these ranges and needn't reach their ends.
Inputs may be any that keep to these rules, and one draw needn't show every extreme that they name: `serve_new`: entries past a slot list's count are filler rows that take no part. `serve_old`: entries past a slot list's count are filler rows that take no part. `count_new`: each device has one owner of its row group, drawn from the seed, whose count is 16. `count_old`: each device has one owner among the devices of its member index, drawn from the seed, whose count is 32.
All inputs are finite; a program needn't handle non-finite values.
Results may differ from the reference program's by a relative error of at most 0.00069.
Values may be sent and summed in bfloat16 or wider, within the bound.
No kernel may reach another device: no remote copies, remote signals or barrier semaphores. Data moves between devices by JAX's collectives and lax.ppermute only.
A program may use at most 32 MiB of HBM per device.

```python
import math
import jax
import jax.numpy as jnp
from jax import lax

D = 768
CAP = 16
CAPG = 32
NEAR = 16
ROWS = 1024
NPTS = 786432
N_GRP = 16
N_SHARD = 48


def draw_points(key, part):
    first, second = jax.random.split(jax.random.fold_in(key, 11))
    base = jax.random.normal(first, (NPTS, D), jnp.float32)
    scales = jnp.exp(jax.random.uniform(second, (NPTS, 1), jnp.float32, math.log(0.5), math.log(2.0)))
    return (base * scales / math.sqrt(D)).astype(jnp.bfloat16)


def draw_counts(key, groups, members, owners, slots):
    first, second, third = jax.random.split(key, 3)
    hotness = jax.random.randint(first, (groups, 1, owners), 1, 5)
    raw = jax.random.randint(second, (groups, members, owners), 0, slots + 1)
    counts = jnp.minimum(slots, raw * hotness // 2)
    full_owner = jax.random.randint(third, (groups, members, 1), 0, owners)
    owner_ids = jnp.arange(owners, dtype=jnp.int32)[None, None, :]
    counts = jnp.where(owner_ids == full_owner, slots, counts)
    return counts.reshape(groups * members * owners, 1).astype(jnp.int32)


def draw_count_new(key, part):
    return draw_counts(jax.random.fold_in(key, 23), N_GRP, N_SHARD, N_SHARD, CAP)


def draw_count_old(key, part):
    return draw_counts(jax.random.fold_in(key, 37), N_GRP, N_SHARD, N_GRP, CAPG)


def touch_ends(values, stream_key, least, top_value):
    place = [jax.random.randint(jax.random.fold_in(stream_key, axis), (), 0, length) for axis, length in enumerate(values.shape)]
    main_axis = values.shape.index(max(values.shape))
    next_to = place[:main_axis] + [(place[main_axis] + 1) % values.shape[main_axis]] + place[main_axis + 1:]
    return values.at[tuple(place)].set(least).at[tuple(next_to)].set(top_value)


def setup_inputs(seed: int = 0) -> dict:
    key_list = jax.random.split(jax.random.key(seed), 6)
    points = draw_points(jax.random.fold_in(key_list[5], 71), 0)
    serve_new = touch_ends(jax.random.randint(key_list[1], (NPTS // ROWS * N_SHARD, CAP), 0, ROWS), jax.random.fold_in(key_list[1], 1), 0, ROWS - 1).astype(jnp.int32)
    serve_old = touch_ends(jax.random.randint(key_list[2], (NPTS // ROWS * N_GRP, CAPG), 0, ROWS), jax.random.fold_in(key_list[2], 1), 0, ROWS - 1).astype(jnp.int32)
    count_new = draw_count_new(jax.random.fold_in(key_list[5], 71), 0)
    count_old = draw_count_old(jax.random.fold_in(key_list[5], 71), 0)
    return {"points": points, "serve_new": serve_new, "serve_old": serve_old, "count_new": count_new, "count_old": count_old}


cap_value = 8.0
far_value = 1.0e9


def join_device(own, candidates, usable):
    own_sq = jnp.sum(jnp.square(own.astype(jnp.float32)), axis=1)
    cand_sq = jnp.sum(jnp.square(candidates.astype(jnp.float32)), axis=1)
    inner = lax.dot_general(candidates, own, (((1,), (1,)), ((), ())), preferred_element_type=jnp.float32)
    distances = cand_sq[:, None] + own_sq[None, :] - 2.0 * inner
    masked = jnp.where(usable[:, None], distances, far_value)
    nearest = jnp.sort(masked.T, axis=1)[:, :NEAR]
    tiles = jnp.where(usable[:, None], distances, cap_value).astype(jnp.bfloat16)
    return nearest, jnp.min(tiles, axis=1).astype(jnp.float32)


def reference(points, serve_new, serve_old, count_new, count_old):
    grid = points.reshape(N_GRP, N_SHARD, ROWS, D)
    served_new = serve_new.reshape(N_GRP, N_SHARD, N_SHARD, CAP)
    served_old = serve_old.reshape(N_GRP, N_SHARD, N_GRP, CAPG)
    counts_new = count_new.reshape(N_GRP, N_SHARD, N_SHARD)
    counts_old = count_old.reshape(N_GRP, N_SHARD, N_GRP)
    owners_new = jnp.arange(N_SHARD, dtype=jnp.int32)[:, None]
    owners_old = jnp.arange(N_GRP, dtype=jnp.int32)[:, None]

    def one_device(index):
        group = index // N_SHARD
        member = index % N_SHARD
        lists_new = served_new[group, :, member, :]
        rows_new = grid[group][owners_new, lists_new]
        lists_old = served_old[:, member, group, :]
        rows_old = grid[:, member][owners_old, lists_old]
        candidates = jnp.concatenate([rows_new.reshape(N_SHARD * CAP, D), rows_old.reshape(N_GRP * CAPG, D)], axis=0)
        usable_new = jnp.arange(CAP, dtype=jnp.int32)[None, :] < counts_new[group, member][:, None]
        usable_old = jnp.arange(CAPG, dtype=jnp.int32)[None, :] < counts_old[group, member][:, None]
        usable = jnp.concatenate([usable_new.reshape(-1), usable_old.reshape(-1)])
        return join_device(grid[group, member], candidates, usable)

    device_ids = jnp.arange(N_GRP * N_SHARD, dtype=jnp.int32)
    nearest_all, minima_all = lax.map(one_device, device_ids)
    minima_new = minima_all[:, :N_SHARD * CAP].reshape(N_GRP, N_SHARD, N_SHARD, CAP).transpose(0, 2, 1, 3)
    minima_old = minima_all[:, N_SHARD * CAP:].reshape(N_GRP, N_SHARD, N_GRP, CAPG).transpose(2, 1, 0, 3)
    served = jnp.concatenate([served_new.reshape(N_GRP * N_SHARD, -1), served_old.reshape(N_GRP * N_SHARD, -1)], axis=1)
    minima = jnp.concatenate([minima_new.reshape(N_GRP * N_SHARD, -1), minima_old.reshape(N_GRP * N_SHARD, -1)], axis=1)
    local_rows = jnp.arange(ROWS, dtype=jnp.int32)

    def one_owner(pair):
        names, values = pair
        matches = names[None, :] == local_rows[:, None]
        return jnp.minimum(cap_value, jnp.min(jnp.where(matches, values[None, :], cap_value), axis=1))

    reverse = lax.map(one_owner, (served, minima))
    return nearest_all.reshape(NPTS, NEAR), reverse.reshape(NPTS)
```

```python
import functools

import jax
import jax.numpy as jnp
from jax import lax
from jax.experimental import pallas as pl
from jax.experimental.pallas import tpu as pltpu
from jax.sharding import PartitionSpec as P

NEAR = 16
LANES = 128
SUBLANES = 8

cap_value = 8.0
far_value = 1000000000.0

VMEM_LIMIT = 48 * 1024 * 1024

SORT16 = (
    (0, 13), (1, 12), (2, 15), (3, 14), (4, 8), (5, 6), (7, 11), (9, 10),
    (0, 5), (1, 7), (2, 9), (3, 4), (6, 13), (8, 14), (10, 15), (11, 12),
    (0, 1), (2, 3), (4, 5), (6, 8), (7, 9), (10, 11), (12, 13), (14, 15),
    (0, 2), (1, 3), (4, 10), (5, 11), (6, 7), (8, 9), (12, 14), (13, 15),
    (1, 2), (3, 12), (4, 6), (5, 7), (8, 10), (9, 11), (13, 14),
    (1, 4), (2, 6), (5, 8), (7, 10), (9, 13), (11, 14),
    (2, 4), (3, 6), (9, 12), (11, 13),
    (3, 5), (6, 8), (7, 9), (10, 12),
    (3, 4), (5, 6), (7, 8), (9, 10), (11, 12),
    (6, 7), (8, 9),
)


def iota(shape, dim):
    return lax.broadcasted_iota(jnp.int32, shape, dim)


def onehot(condition, dtype=jnp.bfloat16):
    return jnp.where(condition, 1.0, 0.0).astype(dtype)


def dot(a, b):
    return lax.dot_general(a, b, (((1,), (0,)), ((), ())), preferred_element_type=jnp.float32)


def flat_parts(start, count, peers, slots, flipped):
    shape = lambda n: (count, n)
    peer = lambda n: iota(shape(n), 1) == (iota(shape(n), 0) + start) // slots
    slot = lambda n: iota(shape(n), 1) == (iota(shape(n), 0) + start) % slots
    return (slot(slots), peer(peers)) if flipped else (peer(peers), slot(slots))


def column(rows_of, lane_of, values):
    picked = dot(onehot(rows_of), values)
    return jnp.sum(jnp.where(lane_of, picked, 0.0), axis=1, keepdims=True)


def index_column(lists, start, count, peers, slots, flipped):
    rows_of, lane_of = flat_parts(start, count, peers, slots, flipped)
    high = column(rows_of, lane_of, (lists // 32).astype(jnp.bfloat16))
    low = column(rows_of, lane_of, (lists % 32).astype(jnp.bfloat16))
    return high.astype(jnp.int32) * 32 + low.astype(jnp.int32)


def gather_kernel(peers, slots, flipped, chunk, points_ref, lists_ref, out_ref):
    rows = points_ref.shape[0]
    for start in range(0, peers * slots, chunk):
        index = index_column(lists_ref[...], start, chunk, peers, slots, flipped)
        picks = onehot(index == iota((chunk, rows), 1))
        out_ref[start : start + chunk, :] = dot(picks, points_ref[...]).astype(jnp.bfloat16)


def gather(points, lists, peers, slots, flipped):
    total = peers * slots
    rows, features = points.shape
    return pl.pallas_call(
        functools.partial(gather_kernel, peers, slots, flipped, 256),
        out_shape=jax.ShapeDtypeStruct((total, features), jnp.bfloat16),
        compiler_params=pltpu.CompilerParams(vmem_limit_bytes=VMEM_LIMIT),
        cost_estimate=pl.CostEstimate(
            flops=2 * total * rows * features, bytes_accessed=2 * (total + rows) * features, transcendentals=0
        ),
    )(points, lists)


def exchange(values, low, high):
    a, b = values[low], values[high]
    values[low], values[high] = jnp.minimum(a, b), jnp.maximum(a, b)


def sort16(values):
    values = list(values)
    for low, high in SORT16:
        exchange(values, low, high)
    return values


def merge16(first, second):
    values = [jnp.minimum(first[k], second[15 - k]) for k in range(16)]
    for gap in (8, 4, 2, 1):
        for k in range(16):
            if not k & gap:
                exchange(values, k, k + gap)
    return values


def block16(ref, start, lanes):
    return [ref[pl.ds(start + SUBLANES * k, SUBLANES), lanes] for k in range(16)]


def smallest16(ref, lanes, held):
    step = 16 * SUBLANES
    first = 0
    if held is None:
        held, first = sort16(block16(ref, 0, lanes)), 1

    def body(t, held):
        start = pl.multiple_of(t * step, step)
        return tuple(merge16(held, sort16(block16(ref, start, lanes))))

    return list(lax.fori_loop(first, ref.shape[0] // step, body, tuple(held)))


def distances_into(dist_ref, minima_ref, cand_ref, points_ref, own_sq_ref, counts_ref, peers, slots, chunk):
    total = peers * slots
    back = jnp.zeros((peers, slots), jnp.float32)
    for start in range(0, total, chunk):
        cand = cand_ref[start : start + chunk, :]
        wide = cand.astype(jnp.float32)
        cand_sq = jnp.sum(wide * wide, axis=1, keepdims=True)
        inner = lax.dot_general(
            cand, points_ref[...], (((1,), (1,)), ((), ())), preferred_element_type=jnp.float32
        )
        dist = cand_sq + own_sq_ref[...] - 2.0 * inner
        peer = iota((chunk, peers), 1) == (iota((chunk, peers), 0) + start) // slots
        count = jnp.sum(jnp.where(peer, counts_ref[...], 0), axis=1, keepdims=True)
        usable = (iota((chunk, 1), 0) + start) % slots < count
        minima = jnp.where(usable, jnp.min(dist, axis=1, keepdims=True), cap_value)
        dist_ref[start : start + chunk, :] = jnp.where(usable, dist, far_value)
        slot = iota((chunk, slots), 1) == (iota((chunk, slots), 0) + start) % slots
        spread = jnp.where(slot, minima, 0.0).astype(jnp.bfloat16)
        owner = iota((peers, chunk), 0) == (iota((peers, chunk), 1) + start) // slots
        back = back + dot(onehot(owner), spread)
    minima_ref[...] = back.astype(jnp.bfloat16)


def near_kernel(peers, slots, chunk, cand_ref, points_ref, own_sq_ref, counts_ref, held_ref, minima_ref, dist_ref):
    distances_into(dist_ref, minima_ref, cand_ref, points_ref, own_sq_ref, counts_ref, peers, slots, chunk)

    def block(t, _):
        lanes = pl.ds(pl.multiple_of(t * LANES, LANES), LANES)
        for k, value in enumerate(smallest16(dist_ref, lanes, None)):
            held_ref[SUBLANES * k : SUBLANES * (k + 1), lanes] = value
        return 0

    lax.fori_loop(0, dist_ref.shape[1] // LANES, block, 0)


def dist_kernel(peers, slots, chunk, cand_ref, points_ref, own_sq_ref, counts_ref, dist_ref, minima_ref):
    distances_into(dist_ref, minima_ref, cand_ref, points_ref, own_sq_ref, counts_ref, peers, slots, chunk)


def select_kernel(dist_ref, held_ref, out_ref):
    held = smallest16(dist_ref, slice(None), block16(held_ref, 0, slice(None)))
    for shift in (4, 2, 1):
        held = merge16(held, [pltpu.roll(value, shift, 0) for value in held])
    sublane = iota((SUBLANES, LANES), 0)
    for half in range(2):
        rows = held[SUBLANES * half]
        for k in range(1, SUBLANES):
            rows = jnp.where(sublane == k, held[SUBLANES * half + k], rows)
        out_ref[SUBLANES * half : SUBLANES * (half + 1), :] = rows


def reverse_kernel(new_lists_ref, old_lists_ref, new_back_ref, old_back_ref, out_ref):
    slots_new, peers_new = new_lists_ref.shape
    peers_old, slots_old = old_lists_ref.shape
    rows = SUBLANES * LANES
    best = jnp.full((1, rows), cap_value, jnp.float32)
    for lists_ref, back_ref, peers, slots, flipped in (
        (new_lists_ref, new_back_ref, peers_new, slots_new, True),
        (old_lists_ref, old_back_ref, peers_old, slots_old, False),
    ):
        chunk = 256
        for start in range(0, peers * slots, chunk):
            index = index_column(lists_ref[...], start, chunk, peers, slots, flipped)
            back = column(*flat_parts(start, chunk, peers, slots, False), back_ref[...])
            matches = index == iota((chunk, rows), 1)
            best = jnp.minimum(best, jnp.min(jnp.where(matches, back, cap_value), axis=0, keepdims=True))
    for k in range(SUBLANES):
        out_ref[k : k + 1, :] = best[:, LANES * k : LANES * (k + 1)]


def body(points, serve_new, serve_old, count_new, count_old):
    rows, features = points.shape
    peers, slots = serve_new.shape
    groups, group_slots = serve_old.shape
    lists_new = serve_new.T
    counts_new, counts_old = count_new.T, count_old.T
    params = pltpu.CompilerParams(vmem_limit_bytes=VMEM_LIMIT)

    offered_old = gather(points, serve_old, groups, group_slots, False)
    offered_new = gather(points, lists_new, peers, slots, True)
    pulled_new = lax.all_to_all(
        offered_new.reshape(peers, slots, features), "shard", split_axis=0, concat_axis=0, tiled=True
    ).reshape(peers * slots, features)
    pulled_old = lax.all_to_all(
        offered_old.reshape(groups, group_slots, features), "grp", split_axis=0, concat_axis=0, tiled=True
    ).reshape(groups * group_slots, features)

    own_sq = jnp.sum(jnp.square(points.astype(jnp.float32)), axis=1)[None, :]

    total_old = groups * group_slots
    held, minima_old = pl.pallas_call(
        functools.partial(near_kernel, groups, group_slots, 256),
        out_shape=(
            jax.ShapeDtypeStruct((16 * SUBLANES, rows), jnp.float32),
            jax.ShapeDtypeStruct((groups, group_slots), jnp.bfloat16),
        ),
        scratch_shapes=[pltpu.VMEM((total_old, rows), jnp.float32)],
        compiler_params=params,
        cost_estimate=pl.CostEstimate(
            flops=8 * total_old * rows * features, bytes_accessed=2 * (total_old + rows) * features, transcendentals=0
        ),
    )(pulled_old, points, own_sq, counts_old)
    back_old = lax.all_to_all(minima_old, "grp", split_axis=0, concat_axis=0, tiled=True)

    total_new = peers * slots
    dist, minima_new = pl.pallas_call(
        functools.partial(dist_kernel, peers, slots, 256),
        out_shape=(
            jax.ShapeDtypeStruct((total_new, rows), jnp.float32),
            jax.ShapeDtypeStruct((peers, slots), jnp.bfloat16),
        ),
        compiler_params=params,
        cost_estimate=pl.CostEstimate(
            flops=2 * total_new * rows * features, bytes_accessed=4 * total_new * rows, transcendentals=0
        ),
    )(pulled_new, points, own_sq, counts_new)
    back_new = lax.all_to_all(minima_new, "shard", split_axis=0, concat_axis=0, tiled=True)

    nearest = pl.pallas_call(
        select_kernel,
        grid=(rows // LANES,),
        in_specs=[
            pl.BlockSpec((total_new, LANES), lambda t: (0, t)),
            pl.BlockSpec((16 * SUBLANES, LANES), lambda t: (0, t)),
        ],
        out_specs=pl.BlockSpec((NEAR, LANES), lambda t: (0, t)),
        out_shape=jax.ShapeDtypeStruct((NEAR, rows), jnp.float32),
        compiler_params=params,
        cost_estimate=pl.CostEstimate(
            flops=8 * total_new * rows * features, bytes_accessed=4 * total_new * rows, transcendentals=0
        ),
    )(dist, held)

    reverse = pl.pallas_call(
        reverse_kernel,
        out_shape=jax.ShapeDtypeStruct((SUBLANES, LANES), jnp.float32),
        compiler_params=params,
    )(lists_new, serve_old, back_new, back_old)
    return nearest.T, reverse.reshape(rows)


def solution(mesh):
    placed = (P(("grp", "shard"), None),) * 5
    return jax.shard_map(
        body,
        mesh=mesh,
        in_specs=placed,
        out_specs=(P(("grp", "shard"), None), P(("grp", "shard"))),
        check_vma=False,
    )
```

```python
import functools

import jax
import jax.numpy as jnp
from jax import lax
from jax.experimental import pallas as pl
from jax.experimental.pallas import tpu as pltpu
from jax.sharding import PartitionSpec as P

NEAR = 16
LANES = 128
SUBLANES = 8

cap_value = 8.0
far_value = 1000000000.0

VMEM_LIMIT = 20 * 1024 * 1024

SORT16 = (
    (0, 13), (1, 12), (2, 15), (3, 14), (4, 8), (5, 6), (7, 11), (9, 10),
    (0, 5), (1, 7), (2, 9), (3, 4), (6, 13), (8, 14), (10, 15), (11, 12),
    (0, 1), (2, 3), (4, 5), (6, 8), (7, 9), (10, 11), (12, 13), (14, 15),
    (0, 2), (1, 3), (4, 10), (5, 11), (6, 7), (8, 9), (12, 14), (13, 15),
    (1, 2), (3, 12), (4, 6), (5, 7), (8, 10), (9, 11), (13, 14),
    (1, 4), (2, 6), (5, 8), (7, 10), (9, 13), (11, 14),
    (2, 4), (3, 6), (9, 12), (11, 13),
    (3, 5), (6, 8), (7, 9), (10, 12),
    (3, 4), (5, 6), (7, 8), (9, 10), (11, 12),
    (6, 7), (8, 9),
)


def iota(shape, dim):
    return lax.broadcasted_iota(jnp.int32, shape, dim)


def onehot(condition, dtype=jnp.bfloat16):
    return jnp.where(condition, 1.0, 0.0).astype(dtype)


def dot(a, b):
    return lax.dot_general(a, b, (((1,), (0,)), ((), ())), preferred_element_type=jnp.float32)


def flat_parts(start, count, peers, slots, order, flipped=False):
    def peer(n):
        return iota((count, n), 1) == order((iota((count, n), 0) + start) // slots)

    def slot(n):
        return iota((count, n), 1) == (iota((count, n), 0) + start) % slots

    return (slot(slots), peer(peers)) if flipped else (peer(peers), slot(slots))


def straight(block):
    return block


def column(rows_of, lane_of, values):
    picked = dot(onehot(rows_of), values)
    return jnp.sum(jnp.where(lane_of, picked, 0.0), axis=1, keepdims=True)


def index_column(lists, parts):
    high = column(*parts, (lists // 32).astype(jnp.bfloat16))
    low = column(*parts, (lists % 32).astype(jnp.bfloat16))
    return high.astype(jnp.int32) * 32 + low.astype(jnp.int32)


def gather_kernel(peers, slots, flipped, chunk, *refs):
    points_ref, lists_ref, place_ref = refs[:3]
    outs = refs[3:]
    rows = points_ref.shape[0]
    order = straight if flipped else lambda block: block ^ place_ref[0]
    size = outs[0].shape[0]
    for start in range(0, peers * slots, chunk):
        index = index_column(lists_ref[...], flat_parts(start, chunk, peers, slots, order, flipped))
        picked = dot(onehot(index == iota((chunk, rows), 1)), points_ref[...]).astype(jnp.bfloat16)
        for at in range(start, start + chunk, min(size, chunk)):
            piece = min(size, chunk)
            outs[at // size][at % size : at % size + piece, :] = picked[at - start : at - start + piece, :]


def gather(points, lists, place, peers, slots, flipped, pieces):
    total = peers * slots
    rows, features = points.shape
    vmem = pl.BlockSpec(memory_space=pltpu.VMEM)
    return pl.pallas_call(
        functools.partial(gather_kernel, peers, slots, flipped, 256),
        in_specs=[vmem, vmem, pl.BlockSpec(memory_space=pltpu.SMEM)],
        out_shape=(jax.ShapeDtypeStruct((total // pieces, features), jnp.bfloat16),) * pieces,
        compiler_params=pltpu.CompilerParams(vmem_limit_bytes=VMEM_LIMIT),
        cost_estimate=pl.CostEstimate(
            flops=2 * total * rows * features, bytes_accessed=2 * (total + rows) * features, transcendentals=0
        ),
    )(points, lists, place)


def exchange(values, low, high):
    a, b = values[low], values[high]
    values[low], values[high] = jnp.minimum(a, b), jnp.maximum(a, b)


def sort16(values):
    values = list(values)
    for low, high in SORT16:
        exchange(values, low, high)
    return values


def merge16(first, second):
    values = [jnp.minimum(first[k], second[15 - k]) for k in range(16)]
    for gap in (8, 4, 2, 1):
        for k in range(16):
            if not k & gap:
                exchange(values, k, k + gap)
    return values


def block16(ref, start, lanes):
    return [ref[pl.ds(start + SUBLANES * k, SUBLANES), lanes] for k in range(16)]


def smallest16(ref, lanes, held):
    step = 16 * SUBLANES
    first = 0
    if held is None:
        held, first = sort16(block16(ref, 0, lanes)), 1

    def body(t, held):
        start = pl.multiple_of(t * step, step)
        return tuple(merge16(held, sort16(block16(ref, start, lanes))))

    return list(lax.fori_loop(first, ref.shape[0] // step, body, tuple(held)))


def distances(cand, points_ref, own_sq_ref):
    wide = cand.astype(jnp.float32)
    cand_sq = jnp.sum(wide * wide, axis=1, keepdims=True)
    inner = lax.dot_general(
        cand, points_ref[...], (((1,), (1,)), ((), ())), preferred_element_type=jnp.float32
    )
    return cand_sq + own_sq_ref[...] - 2.0 * inner


def judge(dist, counts_ref, start, peers, slots, order):
    chunk = dist.shape[0]
    peer_of, slot_of = flat_parts(start, chunk, peers, slots, order)
    count = jnp.sum(jnp.where(peer_of, counts_ref[...], 0), axis=1, keepdims=True)
    usable = (iota((chunk, 1), 0) + start) % slots < count
    minima = jnp.where(usable, jnp.min(dist, axis=1, keepdims=True), cap_value)
    spread = jnp.where(slot_of, minima, 0.0).astype(jnp.bfloat16)
    owner = iota((peers, chunk), 0) == order((iota((peers, chunk), 1) + start) // slots)
    return jnp.where(usable, dist, far_value), dot(onehot(owner), spread)


def near_kernel(groups, slots, *refs):
    count = groups // 2
    evens, (odd_ref, points_ref, own_sq_ref, counts_ref, place_ref) = refs[:count], refs[count : count + 5]
    held_ref, minima_ref, dist_ref = refs[count + 5 :]

    def order(block):
        return jnp.where(block < count, 2 * block, 2 * (block - count) + 1) ^ place_ref[0]

    half = count * slots
    even = jnp.concatenate([ref[:slots, :] for ref in evens], axis=0)
    back = jnp.zeros((groups, slots), jnp.float32)
    for start, cand in ((0, even), (half, odd_ref[...])):
        dist, term = judge(distances(cand, points_ref, own_sq_ref), counts_ref, start, groups, slots, order)
        dist_ref[start : start + half, :] = dist
        back = back + term
    minima_ref[...] = back.astype(jnp.bfloat16)

    def block(t, _):
        lanes = pl.ds(pl.multiple_of(t * LANES, LANES), LANES)
        for k, value in enumerate(smallest16(dist_ref, lanes, None)):
            held_ref[SUBLANES * k : SUBLANES * (k + 1), lanes] = value
        return 0

    lax.fori_loop(0, dist_ref.shape[1] // LANES, block, 0)


def minima_kernel(peers, slots, chunk, cand_ref, points_ref, own_sq_ref, counts_ref, minima_ref):
    back = jnp.zeros((peers, slots), jnp.float32)
    for start in range(0, peers * slots, chunk):
        dist = distances(cand_ref[start : start + chunk, :], points_ref, own_sq_ref)
        back = back + judge(dist, counts_ref, start, peers, slots, straight)[1]
    minima_ref[...] = back.astype(jnp.bfloat16)


def select_kernel(peers, slots, chunk, cand_ref, points_ref, own_sq_ref, counts_ref, held_ref, out_ref, dist_ref):
    for start in range(0, peers * slots, chunk):
        dist = distances(cand_ref[start : start + chunk, :], points_ref, own_sq_ref)
        dist_ref[start : start + chunk, :] = judge(dist, counts_ref, start, peers, slots, straight)[0]
    sublane = iota((SUBLANES, LANES), 0)

    def block(t, _):
        lanes = pl.ds(pl.multiple_of(t * LANES, LANES), LANES)
        held = smallest16(dist_ref, lanes, block16(held_ref, 0, lanes))
        for shift in (4, 2, 1):
            held = merge16(held, [pltpu.roll(value, shift, 0) for value in held])
        for half in range(2):
            rows = held[SUBLANES * half]
            for k in range(1, SUBLANES):
                rows = jnp.where(sublane == k, held[SUBLANES * half + k], rows)
            out_ref[SUBLANES * half : SUBLANES * (half + 1), lanes] = rows
        return 0

    lax.fori_loop(0, dist_ref.shape[1] // LANES, block, 0)


def reverse_kernel(gathered, new_lists_ref, old_lists_ref, new_back_ref, old_back_ref, place_ref, out_ref):
    slots_new, peers_new = new_lists_ref.shape
    groups, slots_old = old_lists_ref.shape
    rows = SUBLANES * LANES
    best = jnp.full((1, rows), cap_value, jnp.float32)
    chunk = 256

    def fold(best, index, back):
        matches = index == iota((chunk, rows), 1)
        return jnp.minimum(best, jnp.min(jnp.where(matches, back, cap_value), axis=0, keepdims=True))

    for start in range(0, groups * slots_old, chunk):
        index = index_column(old_lists_ref[...], flat_parts(start, chunk, groups, slots_old, straight))
        if gathered:
            mine = lambda block: block * groups + place_ref[0]
            parts = flat_parts(start, chunk, groups * groups, slots_old, mine)
        else:
            parts = flat_parts(start, chunk, groups, slots_old, straight)
        best = fold(best, index, column(*parts, old_back_ref[...]))
    for start in range(0, peers_new * slots_new, chunk):
        index = index_column(new_lists_ref[...], flat_parts(start, chunk, peers_new, slots_new, straight, True))
        parts = flat_parts(start, chunk, peers_new, slots_new, straight)
        best = fold(best, index, column(*parts, new_back_ref[...]))
    for k in range(SUBLANES):
        out_ref[k : k + 1, :] = best[:, LANES * k : LANES * (k + 1)]


GATHERED = False


def apart(groups, away):
    return [(g, g ^ away) for g in range(groups)]


def body(points, serve_new, serve_old, count_new, count_old):
    rows, features = points.shape
    peers, slots = serve_new.shape
    groups, group_slots = serve_old.shape
    lists_new = serve_new.T
    counts_new, counts_old = count_new.T, count_old.T
    params = pltpu.CompilerParams(vmem_limit_bytes=VMEM_LIMIT)
    vmem = pl.BlockSpec(memory_space=pltpu.VMEM)
    smem = pl.BlockSpec(memory_space=pltpu.SMEM)
    place = lax.axis_index("grp").astype(jnp.int32).reshape(1)

    (offered_new,) = gather(points, lists_new, place, peers, slots, True, 1)
    pulled_new = lax.all_to_all(
        offered_new.reshape(peers, slots, features), "shard", split_axis=0, concat_axis=0, tiled=True
    ).reshape(peers * slots, features)

    pieces = gather(points, serve_old, place, groups, group_slots, False, groups // 2)
    evens = [pieces[0]] + [
        lax.ppermute(pieces[k], "grp", apart(groups, 2 * k)) for k in range(1, groups // 2)
    ]
    odds = lax.ppermute(
        jnp.concatenate([piece[group_slots:] for piece in evens], axis=0), "grp", apart(groups, 1)
    )

    own_sq = jnp.sum(jnp.square(points.astype(jnp.float32)), axis=1)[None, :]

    total_old = groups * group_slots
    held, minima_old = pl.pallas_call(
        functools.partial(near_kernel, groups, group_slots),
        in_specs=[vmem] * (groups // 2 + 4) + [smem],
        out_shape=(
            jax.ShapeDtypeStruct((16 * SUBLANES, rows), jnp.float32),
            jax.ShapeDtypeStruct((groups, group_slots), jnp.bfloat16),
        ),
        scratch_shapes=[pltpu.VMEM((total_old, rows), jnp.float32)],
        compiler_params=params,
        cost_estimate=pl.CostEstimate(
            flops=2 * total_old * rows * features, bytes_accessed=2 * (total_old + rows) * features, transcendentals=0
        ),
    )(*evens, odds, points, own_sq, counts_old, place)
    pulled_new, minima_old = lax.optimization_barrier((pulled_new, minima_old))
    if GATHERED:
        back_old = lax.all_gather(minima_old, "grp", axis=0, tiled=True)
    else:
        back_old = lax.all_to_all(minima_old, "grp", split_axis=0, concat_axis=0, tiled=True)

    total_new = peers * slots
    minima_new = pl.pallas_call(
        functools.partial(minima_kernel, peers, slots, 256),
        out_shape=jax.ShapeDtypeStruct((peers, slots), jnp.bfloat16),
        compiler_params=params,
        cost_estimate=pl.CostEstimate(
            flops=2 * total_new * rows * features, bytes_accessed=4 * total_new * features, transcendentals=0
        ),
    )(pulled_new, points, own_sq, counts_new)
    back_new = lax.all_to_all(minima_new, "shard", split_axis=0, concat_axis=0, tiled=True)

    pulled_new, _ = lax.optimization_barrier((pulled_new, minima_new))
    nearest = pl.pallas_call(
        functools.partial(select_kernel, peers, slots, 256),
        out_shape=jax.ShapeDtypeStruct((NEAR, rows), jnp.float32),
        scratch_shapes=[pltpu.VMEM((total_new, rows), jnp.float32)],
        compiler_params=params,
        cost_estimate=pl.CostEstimate(
            flops=4 * total_new * rows * features, bytes_accessed=4 * total_new * features, transcendentals=0
        ),
    )(pulled_new, points, own_sq, counts_new, held)

    reverse = pl.pallas_call(
        functools.partial(reverse_kernel, GATHERED),
        in_specs=[vmem] * 4 + [smem],
        out_shape=jax.ShapeDtypeStruct((SUBLANES, LANES), jnp.float32),
        compiler_params=params,
    )(lists_new, serve_old, back_new, back_old, place)
    return nearest.T, reverse.reshape(rows)


def solution(mesh):
    placed = (P(("grp", "shard"), None),) * 5
    return jax.shard_map(
        body,
        mesh=mesh,
        in_specs=placed,
        out_specs=(P(("grp", "shard"), None), P(("grp", "shard"))),
        check_vma=False,
    )
```

```python
import functools

import jax
import jax.numpy as jnp
from jax import lax
from jax.experimental import pallas as pl
from jax.experimental.pallas import tpu as pltpu
from jax.sharding import PartitionSpec as P

NEAR = 16
LANES = 128
SUBLANES = 8

cap_value = 8.0
far_value = 1000000000.0

VMEM_LIMIT = 20 * 1024 * 1024

SORT16 = (
    (0, 13), (1, 12), (2, 15), (3, 14), (4, 8), (5, 6), (7, 11), (9, 10),
    (0, 5), (1, 7), (2, 9), (3, 4), (6, 13), (8, 14), (10, 15), (11, 12),
    (0, 1), (2, 3), (4, 5), (6, 8), (7, 9), (10, 11), (12, 13), (14, 15),
    (0, 2), (1, 3), (4, 10), (5, 11), (6, 7), (8, 9), (12, 14), (13, 15),
    (1, 2), (3, 12), (4, 6), (5, 7), (8, 10), (9, 11), (13, 14),
    (1, 4), (2, 6), (5, 8), (7, 10), (9, 13), (11, 14),
    (2, 4), (3, 6), (9, 12), (11, 13),
    (3, 5), (6, 8), (7, 9), (10, 12),
    (3, 4), (5, 6), (7, 8), (9, 10), (11, 12),
    (6, 7), (8, 9),
)


def iota(shape, dim):
    return lax.broadcasted_iota(jnp.int32, shape, dim)


def onehot(condition, dtype=jnp.bfloat16):
    return jnp.where(condition, 1.0, 0.0).astype(dtype)


def dot(a, b):
    return lax.dot_general(a, b, (((1,), (0,)), ((), ())), preferred_element_type=jnp.float32)


def flat_parts(start, count, peers, slots, order, flipped=False):
    def peer(n):
        return iota((count, n), 1) == order((iota((count, n), 0) + start) // slots)

    def slot(n):
        return iota((count, n), 1) == (iota((count, n), 0) + start) % slots

    return (slot(slots), peer(peers)) if flipped else (peer(peers), slot(slots))


def straight(block):
    return block


def column(rows_of, lane_of, values):
    picked = dot(onehot(rows_of), values)
    return jnp.sum(jnp.where(lane_of, picked, 0.0), axis=1, keepdims=True)


def index_column(lists, parts):
    high = column(*parts, (lists // 32).astype(jnp.bfloat16))
    low = column(*parts, (lists % 32).astype(jnp.bfloat16))
    return high.astype(jnp.int32) * 32 + low.astype(jnp.int32)


def gather_new_kernel(peers, slots, chunk, points_ref, lists_ref, out_ref, points, lists, picked, in_sems, out_sems):
    total, rows = peers * slots, points.shape[0]
    loads = [pltpu.make_async_copy(lists_ref, lists, in_sems.at[0])]
    for k, start in enumerate(range(0, rows, chunk)):
        part = pl.ds(start, chunk)
        loads.append(pltpu.make_async_copy(points_ref.at[part, :], points.at[part, :], in_sems.at[k + 1]))
    for load in loads:
        load.start()
    loads[0].wait()
    index = index_column(lists[...], flat_parts(0, total, peers, slots, straight, True))
    stores = []
    for c, at in enumerate(range(0, total, chunk)):
        acc = None
        for k, start in enumerate(range(0, rows, chunk)):
            if c == 0:
                loads[k + 1].wait()
            picks = onehot(index[at : at + chunk, :] == iota((chunk, chunk), 1) + start)
            term = dot(picks, points[start : start + chunk, :])
            acc = term if acc is None else acc + term
        picked[at : at + chunk, :] = acc.astype(jnp.bfloat16)
        part = pl.ds(at, chunk)
        stores.append(pltpu.make_async_copy(picked.at[part, :], out_ref.at[part, :], out_sems.at[c]))
        stores[-1].start()
    for store in stores:
        store.wait()


def gather_new(points, lists, peers, slots):
    total, chunk = peers * slots, 256
    rows, features = points.shape
    hbm = pl.BlockSpec(memory_space=pltpu.HBM)
    return pl.pallas_call(
        functools.partial(gather_new_kernel, peers, slots, chunk),
        in_specs=[hbm, hbm],
        out_specs=hbm,
        out_shape=pltpu.HBM((total, features), jnp.bfloat16),
        scratch_shapes=[
            pltpu.VMEM((rows, features), jnp.bfloat16),
            pltpu.VMEM(lists.shape, jnp.int32),
            pltpu.VMEM((total, features), jnp.bfloat16),
            pltpu.SemaphoreType.DMA((rows // chunk + 1,)),
            pltpu.SemaphoreType.DMA((total // chunk,)),
        ],
        compiler_params=pltpu.CompilerParams(vmem_limit_bytes=VMEM_LIMIT),
        cost_estimate=pl.CostEstimate(
            flops=2 * total * rows * features, bytes_accessed=2 * (total + rows) * features, transcendentals=0
        ),
    )(pltpu.with_memory_space_constraint(points, pltpu.HBM), pltpu.with_memory_space_constraint(lists, pltpu.HBM))


def gather_old_kernel(groups, slots, chunk, points_ref, lists_ref, place_ref, *outs):
    rows = points_ref.shape[0]
    size = outs[0].shape[0]
    for start in range(0, groups * slots, chunk):
        parts = flat_parts(start, chunk, groups, slots, lambda block: block ^ place_ref[0])
        index = index_column(lists_ref[...], parts)
        picked = dot(onehot(index == iota((chunk, rows), 1)), points_ref[...]).astype(jnp.bfloat16)
        for at in range(0, chunk, size):
            outs[(start + at) // size][...] = picked[at : at + size, :]


def gather_old(points, lists, place, groups, slots, pieces):
    total = groups * slots
    rows, features = points.shape
    vmem = pl.BlockSpec(memory_space=pltpu.VMEM)
    return pl.pallas_call(
        functools.partial(gather_old_kernel, groups, slots, 256),
        in_specs=[vmem, vmem, pl.BlockSpec(memory_space=pltpu.SMEM)],
        out_shape=(jax.ShapeDtypeStruct((total // pieces, features), jnp.bfloat16),) * pieces,
        compiler_params=pltpu.CompilerParams(vmem_limit_bytes=VMEM_LIMIT),
        cost_estimate=pl.CostEstimate(
            flops=2 * total * rows * features, bytes_accessed=2 * (total + rows) * features, transcendentals=0
        ),
    )(points, lists, place)


def exchange(values, low, high):
    a, b = values[low], values[high]
    values[low], values[high] = jnp.minimum(a, b), jnp.maximum(a, b)


def sort16(values):
    values = list(values)
    for low, high in SORT16:
        exchange(values, low, high)
    return values


def merge16(first, second):
    values = [jnp.minimum(first[k], second[15 - k]) for k in range(16)]
    for gap in (8, 4, 2, 1):
        for k in range(16):
            if not k & gap:
                exchange(values, k, k + gap)
    return values


def block16(ref, start, lanes):
    return [ref[pl.ds(start + SUBLANES * k, SUBLANES), lanes] for k in range(16)]


def smallest16(ref, lanes, held):
    step = 16 * SUBLANES
    first = 0
    if held is None:
        held, first = sort16(block16(ref, 0, lanes)), 1

    def body(t, held):
        start = pl.multiple_of(t * step, step)
        return tuple(merge16(held, sort16(block16(ref, start, lanes))))

    return list(lax.fori_loop(first, ref.shape[0] // step, body, tuple(held)))


def distances(cand, points_ref, own_sq_ref):
    wide = cand.astype(jnp.float32)
    cand_sq = jnp.sum(wide * wide, axis=1, keepdims=True)
    inner = lax.dot_general(
        cand, points_ref[...], (((1,), (1,)), ((), ())), preferred_element_type=jnp.float32
    )
    return cand_sq + own_sq_ref[...] - 2.0 * inner


def usable_slots(counts_ref, start, chunk, peers, slots, order):
    peer_of, _ = flat_parts(start, chunk, peers, slots, order)
    count = jnp.sum(jnp.where(peer_of, counts_ref[...], 0), axis=1, keepdims=True)
    return (iota((chunk, 1), 0) + start) % slots < count


def slot_rows(minima, slots):
    chunk = minima.shape[0]
    spread = jnp.where(iota((chunk, slots), 1) == iota((chunk, slots), 0) % slots, minima, 0.0)
    return [jnp.sum(spread[at : at + slots, :], axis=0, keepdims=True) for at in range(0, chunk, slots)]


def near_kernel(groups, slots, *refs):
    count = groups // 2
    evens, (odd_ref, points_ref, own_sq_ref, counts_ref, place_ref) = refs[:count], refs[count : count + 5]
    held_ref, minima_ref, dist_ref = refs[count + 5 :]

    def order(block):
        return jnp.where(block < count, 2 * block, 2 * (block - count) + 1) ^ place_ref[0]

    half = count * slots
    even = jnp.concatenate([ref[:slots, :] for ref in evens], axis=0)
    minima_ref[...] = jnp.zeros_like(minima_ref)
    for start, cand in ((0, even), (half, odd_ref[...])):
        usable = usable_slots(counts_ref, start, half, groups, slots, order)
        dist = distances(cand, points_ref, own_sq_ref)
        dist_ref[start : start + half, :] = jnp.where(usable, dist, far_value)
        minima = jnp.where(usable, jnp.min(dist, axis=1, keepdims=True), cap_value)
        for k, row in enumerate(slot_rows(minima.astype(jnp.bfloat16).astype(jnp.float32), slots)):
            source = order(start // slots + k)
            minima_ref[pl.ds(source * groups + place_ref[0], 1), :] = row

    def block(t, _):
        lanes = pl.ds(pl.multiple_of(t * LANES, LANES), LANES)
        for k, value in enumerate(smallest16(dist_ref, lanes, None)):
            held_ref[SUBLANES * k : SUBLANES * (k + 1), lanes] = value
        return 0

    lax.fori_loop(0, dist_ref.shape[1] // LANES, block, 0)


def minima_kernel(peers, slots, cand_ref, points_ref, own_sq_ref, counts_ref, minima_ref):
    total, rows = peers * slots, points_ref.shape[0]
    cand = cand_ref[...]
    least = None
    for start in range(0, rows, 256):
        part = slice(start, start + 256)
        dist = distances(cand, points_ref.at[part, :], own_sq_ref.at[:, part])
        dist = jnp.minimum(dist[:, :LANES], dist[:, LANES:])
        least = dist if least is None else jnp.minimum(least, dist)
    usable = usable_slots(counts_ref, 0, total, peers, slots, straight)
    minima = jnp.where(usable, jnp.min(least, axis=1, keepdims=True), cap_value)
    for k, row in enumerate(slot_rows(minima, slots)):
        minima_ref[k] = row.astype(jnp.bfloat16)


def select_kernel(peers, slots, chunk, cand_ref, points_ref, own_sq_ref, counts_ref, held_ref, out_ref, dist_ref):
    for start in range(0, peers * slots, chunk):
        usable = usable_slots(counts_ref, start, chunk, peers, slots, straight)
        dist = distances(cand_ref[start : start + chunk, :], points_ref, own_sq_ref)
        dist_ref[start : start + chunk, :] = jnp.where(usable, dist, far_value)
    sublane = iota((SUBLANES, LANES), 0)

    def block(t, _):
        lanes = pl.ds(pl.multiple_of(t * LANES, LANES), LANES)
        held = smallest16(dist_ref, lanes, block16(held_ref, 0, lanes))
        for shift in (4, 2, 1):
            held = merge16(held, [pltpu.roll(value, shift, 0) for value in held])
        for half in range(2):
            rows = held[SUBLANES * half]
            for k in range(1, SUBLANES):
                rows = jnp.where(sublane == k, held[SUBLANES * half + k], rows)
            out_ref[SUBLANES * half : SUBLANES * (half + 1), lanes] = rows
        return 0

    lax.fori_loop(0, dist_ref.shape[1] // LANES, block, 0)


def fold(best, lists, back):
    peers, slots = lists.shape
    for c in range(slots):
        for at in range(0, peers, SUBLANES):
            index = lists[at : at + SUBLANES, c : c + 1]
            value = back[at : at + SUBLANES, c : c + 1]
            best = jnp.where(index == iota(best.shape, 1), jnp.minimum(best, value), best)
    return best


def reverse_old_kernel(lists_ref, back_ref, best_ref):
    best_ref[...] = fold(jnp.full(best_ref.shape, cap_value, jnp.float32), lists_ref[...], back_ref[...])


def reverse_new_kernel(lists_ref, back_ref, best_ref, out_ref):
    back = back_ref[...].reshape(lists_ref.shape).astype(jnp.float32)
    best = jnp.min(fold(best_ref[...], lists_ref[...], back), axis=0, keepdims=True)
    for k in range(SUBLANES):
        out_ref[k : k + 1, :] = best[:, LANES * k : LANES * (k + 1)]


def apart(groups, away):
    return [(g, g ^ away) for g in range(groups)]


def body(points, serve_new, serve_old, count_new, count_old):
    rows, features = points.shape
    peers, slots = serve_new.shape
    groups, group_slots = serve_old.shape
    lists_new = serve_new.T
    counts_new, counts_old = count_new.T, count_old.T
    params = pltpu.CompilerParams(vmem_limit_bytes=VMEM_LIMIT)
    vmem = pl.BlockSpec(memory_space=pltpu.VMEM)
    smem = pl.BlockSpec(memory_space=pltpu.SMEM)
    place = lax.axis_index("grp").astype(jnp.int32).reshape(1)

    offered_new = gather_new(points, lists_new, peers, slots)
    pulled_new = lax.all_to_all(
        offered_new.reshape(peers, slots, features), "shard", split_axis=0, concat_axis=0, tiled=True
    ).reshape(peers * slots, features)

    pieces = gather_old(points, serve_old, place, groups, group_slots, groups // 2)
    evens = [pieces[0]] + [
        lax.ppermute(pieces[k], "grp", apart(groups, 2 * k)) for k in range(1, groups // 2)
    ]
    odds = lax.ppermute(
        jnp.concatenate([piece[group_slots:] for piece in evens], axis=0), "grp", apart(groups, 1)
    )

    own_sq = jnp.sum(jnp.square(points.astype(jnp.float32)), axis=1)[None, :]

    total_old = groups * group_slots
    held, minima_old = pl.pallas_call(
        functools.partial(near_kernel, groups, group_slots),
        in_specs=[vmem] * (groups // 2 + 4) + [smem],
        out_shape=(
            pltpu.HBM((16 * SUBLANES, rows), jnp.float32),
            jax.ShapeDtypeStruct((groups * groups, group_slots), jnp.float32),
        ),
        scratch_shapes=[pltpu.VMEM((total_old, rows), jnp.float32)],
        compiler_params=params,
        cost_estimate=pl.CostEstimate(
            flops=2 * total_old * rows * features, bytes_accessed=2 * (total_old + rows) * features, transcendentals=0
        ),
    )(*evens, odds, points, own_sq, counts_old, place)
    back_old = lax.psum_scatter(minima_old, "grp", scatter_dimension=0, tiled=True)

    total_new = peers * slots
    minima_new = pl.pallas_call(
        functools.partial(minima_kernel, peers, slots),
        out_shape=jax.ShapeDtypeStruct((peers, 1, slots), jnp.bfloat16),
        compiler_params=params,
        cost_estimate=pl.CostEstimate(
            flops=2 * total_new * rows * features, bytes_accessed=4 * total_new * features, transcendentals=0
        ),
    )(pulled_new, points, own_sq, counts_new)
    back_new = lax.all_to_all(minima_new, "shard", split_axis=0, concat_axis=0, tiled=True)

    pulled_new, _ = lax.optimization_barrier((pulled_new, minima_new))
    nearest = pl.pallas_call(
        functools.partial(select_kernel, peers, slots, 256),
        out_shape=jax.ShapeDtypeStruct((NEAR, rows), jnp.float32),
        scratch_shapes=[pltpu.VMEM((total_new, rows), jnp.float32)],
        compiler_params=params,
        cost_estimate=pl.CostEstimate(
            flops=4 * total_new * rows * features, bytes_accessed=4 * total_new * features, transcendentals=0
        ),
    )(pulled_new, points, own_sq, counts_new, held)

    nearest, back_old = lax.optimization_barrier((nearest, back_old))
    best = pl.pallas_call(
        reverse_old_kernel,
        out_shape=jax.ShapeDtypeStruct((SUBLANES, rows), jnp.float32),
        compiler_params=params,
    )(serve_old, back_old)
    reverse = pl.pallas_call(
        reverse_new_kernel,
        out_shape=jax.ShapeDtypeStruct((SUBLANES, LANES), jnp.float32),
        compiler_params=params,
    )(serve_new, back_new, best)
    return nearest.T, reverse.reshape(rows)


def solution(mesh):
    placed = (P(("grp", "shard"), None),) * 5
    return jax.shard_map(
        body,
        mesh=mesh,
        in_specs=placed,
        out_specs=(P(("grp", "shard"), None), P(("grp", "shard"))),
        check_vma=False,
    )
```

```python
import functools

import jax
import jax.numpy as jnp
import numpy as np
from jax import lax
from jax.experimental import pallas as pl
from jax.experimental.pallas import tpu as pltpu
from jax.sharding import PartitionSpec as P

NEAR = 16
LANES = 128
SUBLANES = 8

cap_value = 8.0
far_value = 1000000000.0

VMEM_LIMIT = 20 * 1024 * 1024

SORT16 = (
    (0, 13), (1, 12), (2, 15), (3, 14), (4, 8), (5, 6), (7, 11), (9, 10),
    (0, 5), (1, 7), (2, 9), (3, 4), (6, 13), (8, 14), (10, 15), (11, 12),
    (0, 1), (2, 3), (4, 5), (6, 8), (7, 9), (10, 11), (12, 13), (14, 15),
    (0, 2), (1, 3), (4, 10), (5, 11), (6, 7), (8, 9), (12, 14), (13, 15),
    (1, 2), (3, 12), (4, 6), (5, 7), (8, 10), (9, 11), (13, 14),
    (1, 4), (2, 6), (5, 8), (7, 10), (9, 13), (11, 14),
    (2, 4), (3, 6), (9, 12), (11, 13),
    (3, 5), (6, 8), (7, 9), (10, 12),
    (3, 4), (5, 6), (7, 8), (9, 10), (11, 12),
    (6, 7), (8, 9),
)


def iota(shape, dim):
    return lax.broadcasted_iota(jnp.int32, shape, dim)


def onehot(condition, dtype=jnp.bfloat16):
    return jnp.where(condition, 1.0, 0.0).astype(dtype)


def dot(a, b):
    return lax.dot_general(a, b, (((1,), (0,)), ((), ())), preferred_element_type=jnp.float32)


def flat_parts(start, count, peers, slots, order, flipped=False):
    def peer(n):
        return iota((count, n), 1) == order((iota((count, n), 0) + start) // slots)

    def slot(n):
        return iota((count, n), 1) == (iota((count, n), 0) + start) % slots

    return (slot(slots), peer(peers)) if flipped else (peer(peers), slot(slots))


def straight(block):
    return block


def column(rows_of, lane_of, values):
    picked = dot(onehot(rows_of), values)
    return jnp.sum(jnp.where(lane_of, picked, 0.0), axis=1, keepdims=True)


def index_column(lists, parts):
    high = column(*parts, (lists // 32).astype(jnp.bfloat16))
    low = column(*parts, (lists % 32).astype(jnp.bfloat16))
    return high.astype(jnp.int32) * 32 + low.astype(jnp.int32)


def gather_new_kernel(peers, slots, chunk, points_ref, lists_ref, out_ref, points, lists, picked, in_sems, out_sems):
    total, rows = peers * slots, points.shape[0]
    loads = [pltpu.make_async_copy(lists_ref, lists, in_sems.at[0])]
    for k, start in enumerate(range(0, rows, chunk)):
        part = pl.ds(start, chunk)
        loads.append(pltpu.make_async_copy(points_ref.at[part, :], points.at[part, :], in_sems.at[k + 1]))
    for load in loads:
        load.start()
    loads[0].wait()
    index = index_column(lists[...], flat_parts(0, total, peers, slots, straight, True))
    stores = []
    for c, at in enumerate(range(0, total, chunk)):
        acc = None
        for k, start in enumerate(range(0, rows, chunk)):
            if c == 0:
                loads[k + 1].wait()
            picks = onehot(index[at : at + chunk, :] == iota((chunk, chunk), 1) + start)
            term = dot(picks, points[start : start + chunk, :])
            acc = term if acc is None else acc + term
        picked[at : at + chunk, :] = acc.astype(jnp.bfloat16)
        part = pl.ds(at, chunk)
        stores.append(pltpu.make_async_copy(picked.at[part, :], out_ref.at[part, :], out_sems.at[c]))
        stores[-1].start()
    for store in stores:
        store.wait()


def gather_new(points, lists, peers, slots):
    total, chunk = peers * slots, 256
    rows, features = points.shape
    hbm = pl.BlockSpec(memory_space=pltpu.HBM)
    return pl.pallas_call(
        functools.partial(gather_new_kernel, peers, slots, chunk),
        in_specs=[hbm, hbm],
        out_specs=hbm,
        out_shape=pltpu.HBM((total, features), jnp.bfloat16),
        scratch_shapes=[
            pltpu.VMEM((rows, features), jnp.bfloat16),
            pltpu.VMEM(lists.shape, jnp.int32),
            pltpu.VMEM((total, features), jnp.bfloat16),
            pltpu.SemaphoreType.DMA((rows // chunk + 1,)),
            pltpu.SemaphoreType.DMA((total // chunk,)),
        ],
        compiler_params=pltpu.CompilerParams(vmem_limit_bytes=VMEM_LIMIT),
        cost_estimate=pl.CostEstimate(
            flops=2 * total * rows * features, bytes_accessed=2 * (total + rows) * features, transcendentals=0
        ),
    )(pltpu.with_memory_space_constraint(points, pltpu.HBM), pltpu.with_memory_space_constraint(lists, pltpu.HBM))


def gather_old_kernel(groups, slots, chunk, points_ref, lists_ref, place_ref, *outs):
    rows = points_ref.shape[0]
    size = outs[0].shape[0]
    for start in range(0, groups * slots, chunk):
        parts = flat_parts(start, chunk, groups, slots, lambda block: block ^ place_ref[0])
        index = index_column(lists_ref[...], parts)
        picked = dot(onehot(index == iota((chunk, rows), 1)), points_ref[...]).astype(jnp.bfloat16)
        for at in range(0, chunk, size):
            outs[(start + at) // size][...] = picked[at : at + size, :]


def gather_old(points, lists, place, groups, slots, pieces):
    total = groups * slots
    rows, features = points.shape
    vmem = pl.BlockSpec(memory_space=pltpu.VMEM)
    return pl.pallas_call(
        functools.partial(gather_old_kernel, groups, slots, 256),
        in_specs=[vmem, vmem, pl.BlockSpec(memory_space=pltpu.SMEM)],
        out_shape=(jax.ShapeDtypeStruct((total // pieces, features), jnp.bfloat16),) * pieces,
        compiler_params=pltpu.CompilerParams(vmem_limit_bytes=VMEM_LIMIT),
        cost_estimate=pl.CostEstimate(
            flops=2 * total * rows * features, bytes_accessed=2 * (total + rows) * features, transcendentals=0
        ),
    )(points, lists, place)


def exchange(values, low, high):
    a, b = values[low], values[high]
    values[low], values[high] = jnp.minimum(a, b), jnp.maximum(a, b)


def sort16(values):
    values = list(values)
    for low, high in SORT16:
        exchange(values, low, high)
    return values


def merge16(first, second):
    values = [jnp.minimum(first[k], second[15 - k]) for k in range(16)]
    for gap in (8, 4, 2, 1):
        for k in range(16):
            if not k & gap:
                exchange(values, k, k + gap)
    return values


def block16(ref, start, lanes):
    return [ref[pl.ds(start + SUBLANES * k, SUBLANES), lanes] for k in range(16)]


def smallest16(ref, lanes, held):
    step = 16 * SUBLANES
    first = 0
    if held is None:
        held, first = sort16(block16(ref, 0, lanes)), 1

    def body(t, held):
        start = pl.multiple_of(t * step, step)
        return tuple(merge16(held, sort16(block16(ref, start, lanes))))

    return list(lax.fori_loop(first, ref.shape[0] // step, body, tuple(held)))


def distances(cand, points_ref, own_sq_ref):
    wide = cand.astype(jnp.float32)
    cand_sq = jnp.sum(wide * wide, axis=1, keepdims=True)
    inner = lax.dot_general(
        cand, points_ref[...], (((1,), (1,)), ((), ())), preferred_element_type=jnp.float32
    )
    return cand_sq + own_sq_ref[...] - 2.0 * inner


def usable_slots(counts_ref, start, chunk, peers, slots, order):
    peer_of, _ = flat_parts(start, chunk, peers, slots, order)
    count = jnp.sum(jnp.where(peer_of, counts_ref[...], 0), axis=1, keepdims=True)
    return (iota((chunk, 1), 0) + start) % slots < count


def slot_rows(minima, slots):
    chunk = minima.shape[0]
    spread = jnp.where(iota((chunk, slots), 1) == iota((chunk, slots), 0) % slots, minima, 0.0)
    return [jnp.sum(spread[at : at + slots, :], axis=0, keepdims=True) for at in range(0, chunk, slots)]


def near_kernel(groups, slots, *refs):
    count = groups // 2
    evens, (odd_ref, points_ref, own_sq_ref, counts_ref, place_ref) = refs[:count], refs[count : count + 5]
    held_ref, minima_ref, dist_ref, rows_ref = refs[count + 5 :]

    def order(block):
        return jnp.where(block < count, 2 * block, 2 * (block - count) + 1) ^ place_ref[0]

    half = count * slots
    even = jnp.concatenate([ref[:slots, :] for ref in evens], axis=0)
    for start, cand in ((0, even), (half, odd_ref[...])):
        usable = usable_slots(counts_ref, start, half, groups, slots, order)
        dist = distances(cand, points_ref, own_sq_ref)
        dist_ref[start : start + half, :] = jnp.where(usable, dist, far_value)
        minima = jnp.where(usable, jnp.min(dist, axis=1, keepdims=True), cap_value)
        for k, row in enumerate(slot_rows(minima, slots)):
            at = 2 * k + (start > 0)
            rows_ref[at : at + 1, :] = row
    minima_ref[...] = rows_ref[...].astype(jnp.bfloat16)

    def block(t, _):
        lanes = pl.ds(pl.multiple_of(t * LANES, LANES), LANES)
        for k, value in enumerate(smallest16(dist_ref, lanes, None)):
            held_ref[SUBLANES * k : SUBLANES * (k + 1), lanes] = value
        return 0

    lax.fori_loop(0, dist_ref.shape[1] // LANES, block, 0)


def minima_kernel(peers, slots, cand_ref, points_ref, own_sq_ref, counts_ref, minima_ref):
    total, rows = peers * slots, points_ref.shape[0]
    cand = cand_ref[...]
    wide = cand.astype(jnp.float32)
    cand_sq = jnp.sum(wide * wide, axis=1, keepdims=True)
    least = None
    for start in range(0, rows, 256):
        inner = lax.dot_general(
            cand, points_ref[start : start + 256, :], (((1,), (1,)), ((), ())), preferred_element_type=jnp.float32
        )
        for at in range(0, 256, LANES):
            own = own_sq_ref[:, start + at : start + at + LANES]
            dist = cand_sq + own - 2.0 * inner[:, at : at + LANES]
            least = dist if least is None else jnp.minimum(least, dist)
    usable = usable_slots(counts_ref, 0, total, peers, slots, straight)
    minima = jnp.where(usable, jnp.min(least, axis=1, keepdims=True), cap_value)
    for k, row in enumerate(slot_rows(minima, slots)):
        minima_ref[k] = row.astype(jnp.bfloat16)


def select_kernel(peers, slots, first, done, *refs):
    cand_ref, points_ref, own_sq_ref, counts_ref, held_ref = refs[:5]
    parts, (out_ref, dist_ref) = refs[5 : 5 + done], refs[5 + done :]
    total, rows = dist_ref.shape
    chunk = 256
    for start in range(0, total, chunk):
        usable = usable_slots(counts_ref, start, chunk, peers, slots, straight)
        points, own = points_ref.at[first : first + rows, :], own_sq_ref.at[:, first : first + rows]
        dist = distances(cand_ref[start : start + chunk, :], points, own)
        dist_ref[start : start + chunk, :] = jnp.where(usable, dist, far_value)
    sublane = iota((SUBLANES, LANES), 0)
    for k, part in enumerate(parts):
        out_ref[:, k * rows : (k + 1) * rows] = part[...]
    shift_out = done * rows

    def block(t, _):
        lanes = pl.ds(pl.multiple_of(t * LANES, LANES), LANES)
        there = pl.ds(pl.multiple_of(t * LANES + first, LANES), LANES)
        held = smallest16(dist_ref, lanes, block16(held_ref, 0, there))
        for shift in (4, 2, 1):
            held = merge16(held, [pltpu.roll(value, shift, 0) for value in held])
        for half in range(2):
            near = held[SUBLANES * half]
            for k in range(1, SUBLANES):
                near = jnp.where(sublane == k, held[SUBLANES * half + k], near)
            out_lanes = pl.ds(pl.multiple_of(t * LANES + shift_out, LANES), LANES)
            out_ref[SUBLANES * half : SUBLANES * (half + 1), out_lanes] = near
        return 0

    lax.fori_loop(0, rows // LANES, block, 0)


def fold(best, lists, back):
    peers, slots = lists.shape
    for c in range(slots):
        for at in range(0, peers, SUBLANES):
            index = lists[at : at + SUBLANES, c : c + 1]
            value = back[at : at + SUBLANES, c : c + 1]
            best = jnp.where(index == iota(best.shape, 1), jnp.minimum(best, value), best)
    return best


def reverse_old_kernel(bit, lists_ref, kept_ref, came_ref, place_ref, best_ref):
    groups = lists_ref.shape[0]
    back = jnp.where(iota(kept_ref.shape, 0) & bit != 0, came_ref[...].astype(jnp.float32), kept_ref[...].astype(jnp.float32))
    rows_of = iota((groups, groups), 1) == iota((groups, groups), 0) ^ place_ref[0]
    back = dot(onehot(rows_of), back.astype(jnp.bfloat16))
    best_ref[...] = fold(jnp.full(best_ref.shape, cap_value, jnp.float32), lists_ref[...], back)


def reverse_new_kernel(lists_ref, back_ref, best_ref, out_ref):
    back = back_ref[...].reshape(lists_ref.shape).astype(jnp.float32)
    best = jnp.min(fold(best_ref[...], lists_ref[...], back), axis=0, keepdims=True)
    for k in range(SUBLANES):
        out_ref[k : k + 1, :] = best[:, LANES * k : LANES * (k + 1)]


def apart(groups, away):
    return [(g, g ^ away) for g in range(groups)]


def body(points, serve_new, serve_old, count_new, count_old):
    rows, features = points.shape
    peers, slots = serve_new.shape
    groups, group_slots = serve_old.shape
    lists_new = serve_new.T
    counts_new, counts_old = count_new.T, count_old.T
    params = pltpu.CompilerParams(vmem_limit_bytes=VMEM_LIMIT)
    vmem = pl.BlockSpec(memory_space=pltpu.VMEM)
    smem = pl.BlockSpec(memory_space=pltpu.SMEM)
    place = lax.axis_index("grp").astype(jnp.int32).reshape(1)

    offered_new = gather_new(points, lists_new, peers, slots)
    pulled_new = lax.all_to_all(
        offered_new.reshape(peers, slots, features), "shard", split_axis=0, concat_axis=0, tiled=True
    ).reshape(peers * slots, features)

    pieces = gather_old(points, serve_old, place, groups, group_slots, groups // 2)
    evens = [pieces[0]] + [
        lax.ppermute(pieces[k], "grp", apart(groups, 2 * k)) for k in range(1, groups // 2)
    ]
    odds = lax.ppermute(
        jnp.concatenate([piece[group_slots:] for piece in evens], axis=0), "grp", apart(groups, 1)
    )

    own_sq = jnp.sum(jnp.square(points.astype(jnp.float32)), axis=1)[None, :]

    total_old = groups * group_slots
    held, minima_old = pl.pallas_call(
        functools.partial(near_kernel, groups, group_slots),
        in_specs=[vmem] * (groups // 2 + 4) + [smem],
        out_shape=(
            jax.ShapeDtypeStruct((16 * SUBLANES, rows), jnp.float32),
            jax.ShapeDtypeStruct((groups, group_slots), jnp.bfloat16),
        ),
        scratch_shapes=[
            pltpu.VMEM((total_old, rows), jnp.float32),
            pltpu.VMEM((groups, group_slots), jnp.float32),
        ],
        compiler_params=params,
        cost_estimate=pl.CostEstimate(
            flops=2 * total_old * rows * features, bytes_accessed=2 * (total_old + rows) * features, transcendentals=0
        ),
    )(*evens, odds, points, own_sq, counts_old, place)
    total_new = peers * slots
    minima_new = pl.pallas_call(
        functools.partial(minima_kernel, peers, slots),
        out_shape=jax.ShapeDtypeStruct((peers, 1, slots), jnp.bfloat16),
        compiler_params=params,
        cost_estimate=pl.CostEstimate(
            flops=2 * total_new * rows * features, bytes_accessed=4 * total_new * features, transcendentals=0
        ),
    )(pulled_new, points, own_sq, counts_new)
    back_new = lax.all_to_all(minima_new, "shard", split_axis=0, concat_axis=0, tiled=True)

    pulled_new, kept, _ = lax.optimization_barrier((pulled_new, minima_old, minima_new))
    steps = groups.bit_length() - 1
    part = rows // steps
    nearest = []
    for step in range(steps):
        bit = 1 << step
        came = lax.ppermute(kept, "grp", apart(groups, bit))
        last = step == steps - 1
        nearest.append(
            pl.pallas_call(
                functools.partial(select_kernel, peers, slots, step * part, step if last else 0),
                out_shape=jax.ShapeDtypeStruct((NEAR, rows if last else part), jnp.float32),
                scratch_shapes=[pltpu.VMEM((total_new, part), jnp.float32)],
                compiler_params=params,
                cost_estimate=pl.CostEstimate(
                    flops=2 * total_new * rows * features, bytes_accessed=4 * total_new * features, transcendentals=0
                ),
            )(pulled_new, points, own_sq, counts_new, held, *(nearest if last else []))
        )
        if not last:
            kept = jnp.where(np.arange(groups)[:, None] & np.full(group_slots, bit) != 0, came, kept)
            kept, pulled_new = lax.optimization_barrier((kept, pulled_new))
    nearest = nearest[-1]

    best = pl.pallas_call(
        functools.partial(reverse_old_kernel, bit),
        in_specs=[vmem] * 3 + [smem],
        out_shape=jax.ShapeDtypeStruct((SUBLANES, rows), jnp.float32),
        compiler_params=params,
    )(serve_old, kept, came, place)
    reverse = pl.pallas_call(
        reverse_new_kernel,
        out_shape=jax.ShapeDtypeStruct((SUBLANES, LANES), jnp.float32),
        compiler_params=params,
    )(serve_new, back_new, best)
    return nearest.T, reverse.reshape(rows)


def solution(mesh):
    placed = (P(("grp", "shard"), None),) * 5
    return jax.shard_map(
        body,
        mesh=mesh,
        in_specs=placed,
        out_specs=(P(("grp", "shard"), None), P(("grp", "shard"))),
        check_vma=False,
    )
```

```python
import functools

import jax
import jax.numpy as jnp
from jax import lax
from jax.experimental import pallas as pl
from jax.experimental.pallas import tpu as pltpu
from jax.sharding import PartitionSpec as P

NEAR = 16
LANES = 128
SUBLANES = 8

cap_value = 8.0
far_value = 1000000000.0

VMEM_LIMIT = 20 * 1024 * 1024

SORT16 = (
    (0, 13), (1, 12), (2, 15), (3, 14), (4, 8), (5, 6), (7, 11), (9, 10),
    (0, 5), (1, 7), (2, 9), (3, 4), (6, 13), (8, 14), (10, 15), (11, 12),
    (0, 1), (2, 3), (4, 5), (6, 8), (7, 9), (10, 11), (12, 13), (14, 15),
    (0, 2), (1, 3), (4, 10), (5, 11), (6, 7), (8, 9), (12, 14), (13, 15),
    (1, 2), (3, 12), (4, 6), (5, 7), (8, 10), (9, 11), (13, 14),
    (1, 4), (2, 6), (5, 8), (7, 10), (9, 13), (11, 14),
    (2, 4), (3, 6), (9, 12), (11, 13),
    (3, 5), (6, 8), (7, 9), (10, 12),
    (3, 4), (5, 6), (7, 8), (9, 10), (11, 12),
    (6, 7), (8, 9),
)


def iota(shape, dim):
    return lax.broadcasted_iota(jnp.int32, shape, dim)


def onehot(condition, dtype=jnp.bfloat16):
    return jnp.where(condition, 1.0, 0.0).astype(dtype)


def dot(a, b):
    return lax.dot_general(a, b, (((1,), (0,)), ((), ())), preferred_element_type=jnp.float32)


def flat_parts(start, count, peers, slots, order, flipped=False):
    def peer(n):
        return iota((count, n), 1) == order((iota((count, n), 0) + start) // slots)

    def slot(n):
        return iota((count, n), 1) == (iota((count, n), 0) + start) % slots

    return (slot(slots), peer(peers)) if flipped else (peer(peers), slot(slots))


def straight(block):
    return block


def column(rows_of, lane_of, values):
    picked = dot(onehot(rows_of), values)
    return jnp.sum(jnp.where(lane_of, picked, 0.0), axis=1, keepdims=True)


def index_column(lists, parts):
    high = column(*parts, (lists // 32).astype(jnp.bfloat16))
    low = column(*parts, (lists % 32).astype(jnp.bfloat16))
    return high.astype(jnp.int32) * 32 + low.astype(jnp.int32)


def gather_new_kernel(peers, slots, chunk, points_ref, lists_ref, out_ref, points, lists, picked, in_sems, out_sems):
    total, rows = peers * slots, points.shape[0]
    loads = [pltpu.make_async_copy(lists_ref, lists, in_sems.at[0])]
    for k, start in enumerate(range(0, rows, chunk)):
        part = pl.ds(start, chunk)
        loads.append(pltpu.make_async_copy(points_ref.at[part, :], points.at[part, :], in_sems.at[k + 1]))
    for load in loads:
        load.start()
    loads[0].wait()
    index = index_column(lists[...], flat_parts(0, total, peers, slots, straight, True))
    stores = []
    for c, at in enumerate(range(0, total, chunk)):
        acc = None
        for k, start in enumerate(range(0, rows, chunk)):
            if c == 0:
                loads[k + 1].wait()
            picks = onehot(index[at : at + chunk, :] == iota((chunk, chunk), 1) + start)
            term = dot(picks, points[start : start + chunk, :])
            acc = term if acc is None else acc + term
        picked[at : at + chunk, :] = acc.astype(jnp.bfloat16)
        part = pl.ds(at, chunk)
        stores.append(pltpu.make_async_copy(picked.at[part, :], out_ref.at[part, :], out_sems.at[c]))
        stores[-1].start()
    for store in stores:
        store.wait()


def gather_new(points, lists, peers, slots):
    total, chunk = peers * slots, 256
    rows, features = points.shape
    hbm = pl.BlockSpec(memory_space=pltpu.HBM)
    return pl.pallas_call(
        functools.partial(gather_new_kernel, peers, slots, chunk),
        in_specs=[hbm, hbm],
        out_specs=hbm,
        out_shape=pltpu.HBM((total, features), jnp.bfloat16),
        scratch_shapes=[
            pltpu.VMEM((rows, features), jnp.bfloat16),
            pltpu.VMEM(lists.shape, jnp.int32),
            pltpu.VMEM((total, features), jnp.bfloat16),
            pltpu.SemaphoreType.DMA((rows // chunk + 1,)),
            pltpu.SemaphoreType.DMA((total // chunk,)),
        ],
        compiler_params=pltpu.CompilerParams(vmem_limit_bytes=VMEM_LIMIT),
        cost_estimate=pl.CostEstimate(
            flops=2 * total * rows * features, bytes_accessed=2 * (total + rows) * features, transcendentals=0
        ),
    )(pltpu.with_memory_space_constraint(points, pltpu.HBM), pltpu.with_memory_space_constraint(lists, pltpu.HBM))


def gather_old_kernel(groups, slots, chunk, points_ref, lists_ref, place_ref, *outs):
    rows = points_ref.shape[0]
    size = outs[0].shape[0]
    for start in range(0, groups * slots, chunk):
        parts = flat_parts(start, chunk, groups, slots, lambda block: block ^ place_ref[0])
        index = index_column(lists_ref[...], parts)
        picked = dot(onehot(index == iota((chunk, rows), 1)), points_ref[...]).astype(jnp.bfloat16)
        for at in range(0, chunk, size):
            outs[(start + at) // size][...] = picked[at : at + size, :]


def gather_old(points, lists, place, groups, slots, pieces):
    total = groups * slots
    rows, features = points.shape
    vmem = pl.BlockSpec(memory_space=pltpu.VMEM)
    return pl.pallas_call(
        functools.partial(gather_old_kernel, groups, slots, 256),
        in_specs=[vmem, vmem, pl.BlockSpec(memory_space=pltpu.SMEM)],
        out_shape=(jax.ShapeDtypeStruct((total // pieces, features), jnp.bfloat16),) * pieces,
        compiler_params=pltpu.CompilerParams(vmem_limit_bytes=VMEM_LIMIT),
        cost_estimate=pl.CostEstimate(
            flops=2 * total * rows * features, bytes_accessed=2 * (total + rows) * features, transcendentals=0
        ),
    )(points, lists, place)


def exchange(values, low, high):
    a, b = values[low], values[high]
    values[low], values[high] = jnp.minimum(a, b), jnp.maximum(a, b)


def sort16(values):
    values = list(values)
    for low, high in SORT16:
        exchange(values, low, high)
    return values


def merge16(first, second):
    values = [jnp.minimum(first[k], second[15 - k]) for k in range(16)]
    for gap in (8, 4, 2, 1):
        for k in range(16):
            if not k & gap:
                exchange(values, k, k + gap)
    return values


def block16(ref, start, lanes):
    return [ref[pl.ds(start + SUBLANES * k, SUBLANES), lanes] for k in range(16)]


def smallest16(ref, lanes, held):
    step = 16 * SUBLANES
    first = 0
    if held is None:
        held, first = sort16(block16(ref, 0, lanes)), 1

    def body(t, held):
        start = pl.multiple_of(t * step, step)
        return tuple(merge16(held, sort16(block16(ref, start, lanes))))

    return list(lax.fori_loop(first, ref.shape[0] // step, body, tuple(held)))


def distances(cand, points_ref, own_sq_ref):
    wide = cand.astype(jnp.float32)
    cand_sq = jnp.sum(wide * wide, axis=1, keepdims=True)
    inner = lax.dot_general(
        cand, points_ref[...], (((1,), (1,)), ((), ())), preferred_element_type=jnp.float32
    )
    return cand_sq + own_sq_ref[...] - 2.0 * inner


def usable_slots(counts_ref, start, chunk, peers, slots, order):
    peer_of, _ = flat_parts(start, chunk, peers, slots, order)
    count = jnp.sum(jnp.where(peer_of, counts_ref[...], 0), axis=1, keepdims=True)
    return (iota((chunk, 1), 0) + start) % slots < count


def slot_rows(minima, slots):
    chunk = minima.shape[0]
    spread = jnp.where(iota((chunk, slots), 1) == iota((chunk, slots), 0) % slots, minima, 0.0)
    return [jnp.sum(spread[at : at + slots, :], axis=0, keepdims=True) for at in range(0, chunk, slots)]


def halves_kernel(slots, *refs):
    pieces, (mine_ref, handed_ref) = refs[:-2], refs[-2:]
    for k, piece in enumerate(pieces):
        mine_ref[k * slots : (k + 1) * slots, :] = piece[:slots, :]
        handed_ref[k * slots : (k + 1) * slots, :] = piece[slots:, :]


def near_kernel(
    groups, slots, even_ref, odd_ref, points_ref, own_sq_ref, counts_ref, place_ref,
    held_ref, minima_ref, dist_ref, held, sems,
):
    count = groups // 2
    half = count * slots

    def order(block):
        return jnp.where(block < count, 2 * block, 2 * (block - count) + 1) ^ place_ref[0]

    for start, cand_ref in ((0, even_ref), (half, odd_ref)):
        usable = usable_slots(counts_ref, start, half, groups, slots, order)
        dist = distances(cand_ref[...], points_ref, own_sq_ref)
        dist_ref[start : start + half, :] = jnp.where(usable, dist, far_value)
        minima = jnp.where(usable, jnp.min(dist, axis=1, keepdims=True), cap_value)
        for k, row in enumerate(slot_rows(minima, slots)):
            minima_ref[order(start // slots + k)] = row.astype(jnp.bfloat16)

    def block(t, _):
        lanes = pl.ds(pl.multiple_of(t * LANES, LANES), LANES)
        for k, value in enumerate(smallest16(dist_ref, lanes, None)):
            held[SUBLANES * k : SUBLANES * (k + 1), lanes] = value
        return 0

    blocks = dist_ref.shape[1] // LANES
    copies = []
    for part in range(2):
        first, last = part * blocks // 2, (part + 1) * blocks // 2
        lax.fori_loop(first, last, block, 0)
        lanes = pl.ds(first * LANES, (last - first) * LANES)
        copies.append(pltpu.make_async_copy(held.at[:, lanes], held_ref.at[:, lanes], sems.at[part]))
        copies[-1].start()
    for copy in copies:
        copy.wait()


def minima_kernel(peers, slots, cand_ref, points_ref, own_sq_ref, counts_ref, minima_ref):
    total, rows = peers * slots, points_ref.shape[0]
    cand = cand_ref[...]
    wide = cand.astype(jnp.float32)
    cand_sq = jnp.sum(wide * wide, axis=1, keepdims=True)
    least = None
    for start in range(0, rows, 256):
        inner = lax.dot_general(
            cand, points_ref[start : start + 256, :], (((1,), (1,)), ((), ())), preferred_element_type=jnp.float32
        )
        for at in range(0, 256, LANES):
            own = own_sq_ref[:, start + at : start + at + LANES]
            dist = cand_sq + own - 2.0 * inner[:, at : at + LANES]
            least = dist if least is None else jnp.minimum(least, dist)
    usable = usable_slots(counts_ref, 0, total, peers, slots, straight)
    minima = jnp.where(usable, jnp.min(least, axis=1, keepdims=True), cap_value)
    for k, row in enumerate(slot_rows(minima, slots)):
        minima_ref[k] = row.astype(jnp.bfloat16)


def select_kernel(
    peers, slots, chunk, cand_ref, points_ref, own_sq_ref, counts_ref, held_hbm_ref, out_ref, dist_ref, held_ref, sem
):
    fetch = pltpu.make_async_copy(held_hbm_ref, held_ref, sem)
    fetch.start()
    for start in range(0, peers * slots, chunk):
        usable = usable_slots(counts_ref, start, chunk, peers, slots, straight)
        dist = distances(cand_ref[start : start + chunk, :], points_ref, own_sq_ref)
        dist_ref[start : start + chunk, :] = jnp.where(usable, dist, far_value)
    fetch.wait()
    sublane = iota((SUBLANES, LANES), 0)

    def block(t, _):
        lanes = pl.ds(pl.multiple_of(t * LANES, LANES), LANES)
        held = smallest16(dist_ref, lanes, block16(held_ref, 0, lanes))
        for shift in (4, 2, 1):
            held = merge16(held, [pltpu.roll(value, shift, 0) for value in held])
        for half in range(2):
            rows = held[SUBLANES * half]
            for k in range(1, SUBLANES):
                rows = jnp.where(sublane == k, held[SUBLANES * half + k], rows)
            out_ref[SUBLANES * half : SUBLANES * (half + 1), lanes] = rows
        return 0

    lax.fori_loop(0, dist_ref.shape[1] // LANES, block, 0)


def fold(best, lists, back):
    peers, slots = lists.shape
    for c in range(slots):
        for at in range(0, peers, SUBLANES):
            index = lists[at : at + SUBLANES, c : c + 1]
            value = back[at : at + SUBLANES, c : c + 1]
            best = jnp.where(index == iota(best.shape, 1), jnp.minimum(best, value), best)
    return best


def reverse_kernel(new_lists_ref, old_lists_ref, new_back_ref, old_back_ref, out_ref):
    best = jnp.full((SUBLANES, SUBLANES * LANES), cap_value, jnp.float32)
    for lists_ref, back_ref in ((old_lists_ref, old_back_ref), (new_lists_ref, new_back_ref)):
        best = fold(best, lists_ref[...], back_ref[...].reshape(lists_ref.shape).astype(jnp.float32))
    best = jnp.min(best, axis=0, keepdims=True)
    for k in range(SUBLANES):
        out_ref[k : k + 1, :] = best[:, LANES * k : LANES * (k + 1)]


def apart(groups, away):
    return [(g, g ^ away) for g in range(groups)]


def body(points, serve_new, serve_old, count_new, count_old):
    rows, features = points.shape
    peers, slots = serve_new.shape
    groups, group_slots = serve_old.shape
    lists_new = serve_new.T
    counts_new, counts_old = count_new.T, count_old.T
    params = pltpu.CompilerParams(vmem_limit_bytes=VMEM_LIMIT)
    vmem = pl.BlockSpec(memory_space=pltpu.VMEM)
    smem = pl.BlockSpec(memory_space=pltpu.SMEM)
    place = lax.axis_index("grp").astype(jnp.int32).reshape(1)

    offered_new = gather_new(points, lists_new, peers, slots)
    pulled_new = lax.all_to_all(
        offered_new.reshape(peers, slots, features), "shard", split_axis=0, concat_axis=0, tiled=True
    ).reshape(peers * slots, features)

    pieces = gather_old(points, serve_old, place, groups, group_slots, groups // 2)
    came = {0: pieces[0]}
    for k in sorted(range(1, groups // 2), key=lambda k: min(k, groups // 2 - k), reverse=True):
        came[k] = lax.ppermute(pieces[k], "grp", apart(groups, 2 * k))
    evens = [came[k] for k in range(groups // 2)]
    half = groups // 2 * group_slots
    evens, handed = pl.pallas_call(
        functools.partial(halves_kernel, group_slots),
        out_shape=(jax.ShapeDtypeStruct((half, features), jnp.bfloat16),) * 2,
        compiler_params=params,
        cost_estimate=pl.CostEstimate(flops=0, bytes_accessed=8 * half * features, transcendentals=0),
    )(*evens)
    odds = lax.ppermute(handed, "grp", apart(groups, 1))

    own_sq = jnp.sum(jnp.square(points.astype(jnp.float32)), axis=1)[None, :]

    total_old = groups * group_slots
    held, minima_old = pl.pallas_call(
        functools.partial(near_kernel, groups, group_slots),
        in_specs=[vmem] * 5 + [smem],
        out_specs=(pl.BlockSpec(memory_space=pltpu.HBM), vmem),
        out_shape=(
            pltpu.HBM((16 * SUBLANES, rows), jnp.float32),
            jax.ShapeDtypeStruct((groups, 1, group_slots), jnp.bfloat16),
        ),
        scratch_shapes=[
            pltpu.VMEM((total_old, rows), jnp.float32),
            pltpu.VMEM((16 * SUBLANES, rows), jnp.float32),
            pltpu.SemaphoreType.DMA((2,)),
        ],
        compiler_params=params,
        cost_estimate=pl.CostEstimate(
            flops=2 * total_old * rows * features, bytes_accessed=2 * (total_old + rows) * features, transcendentals=0
        ),
    )(evens, odds, points, own_sq, counts_old, place)
    pulled_new, minima_old = lax.optimization_barrier((pulled_new, minima_old))
    back_old = lax.all_to_all(minima_old, "grp", split_axis=0, concat_axis=0, tiled=True)

    total_new = peers * slots
    minima_new = pl.pallas_call(
        functools.partial(minima_kernel, peers, slots),
        out_shape=jax.ShapeDtypeStruct((peers, 1, slots), jnp.bfloat16),
        compiler_params=params,
        cost_estimate=pl.CostEstimate(
            flops=2 * total_new * rows * features, bytes_accessed=4 * total_new * features, transcendentals=0
        ),
    )(pulled_new, points, own_sq, counts_new)
    back_new = lax.all_to_all(minima_new, "shard", split_axis=0, concat_axis=0, tiled=True)

    pulled_new, _ = lax.optimization_barrier((pulled_new, minima_new))
    nearest = pl.pallas_call(
        functools.partial(select_kernel, peers, slots, 256),
        in_specs=[vmem] * 4 + [pl.BlockSpec(memory_space=pltpu.HBM)],
        out_shape=jax.ShapeDtypeStruct((NEAR, rows), jnp.float32),
        scratch_shapes=[
            pltpu.VMEM((total_new, rows), jnp.float32),
            pltpu.VMEM((16 * SUBLANES, rows), jnp.float32),
            pltpu.SemaphoreType.DMA,
        ],
        compiler_params=params,
        cost_estimate=pl.CostEstimate(
            flops=4 * total_new * rows * features, bytes_accessed=4 * total_new * features, transcendentals=0
        ),
    )(pulled_new, points, own_sq, counts_new, pltpu.with_memory_space_constraint(held, pltpu.HBM))

    reverse = pl.pallas_call(
        reverse_kernel,
        out_shape=jax.ShapeDtypeStruct((SUBLANES, LANES), jnp.float32),
        compiler_params=params,
    )(serve_new, serve_old, back_new, back_old)
    return nearest.T, reverse.reshape(rows)


def solution(mesh):
    placed = (P(("grp", "shard"), None),) * 5
    return jax.shard_map(
        body,
        mesh=mesh,
        in_specs=placed,
        out_specs=(P(("grp", "shard"), None), P(("grp", "shard"))),
        check_vma=False,
    )
```

```python
import functools

import jax
import jax.numpy as jnp
from jax import lax
from jax.experimental import pallas as pl
from jax.experimental.pallas import tpu as pltpu
from jax.sharding import PartitionSpec as P

NEAR = 16
LANES = 128
SUBLANES = 8

cap_value = 8.0
far_value = 1000000000.0

VMEM_LIMIT = 20 * 1024 * 1024

SORT16 = (
    (0, 13), (1, 12), (2, 15), (3, 14), (4, 8), (5, 6), (7, 11), (9, 10),
    (0, 5), (1, 7), (2, 9), (3, 4), (6, 13), (8, 14), (10, 15), (11, 12),
    (0, 1), (2, 3), (4, 5), (6, 8), (7, 9), (10, 11), (12, 13), (14, 15),
    (0, 2), (1, 3), (4, 10), (5, 11), (6, 7), (8, 9), (12, 14), (13, 15),
    (1, 2), (3, 12), (4, 6), (5, 7), (8, 10), (9, 11), (13, 14),
    (1, 4), (2, 6), (5, 8), (7, 10), (9, 13), (11, 14),
    (2, 4), (3, 6), (9, 12), (11, 13),
    (3, 5), (6, 8), (7, 9), (10, 12),
    (3, 4), (5, 6), (7, 8), (9, 10), (11, 12),
    (6, 7), (8, 9),
)


def iota(shape, dim):
    return lax.broadcasted_iota(jnp.int32, shape, dim)


def onehot(condition, dtype=jnp.bfloat16):
    return jnp.where(condition, 1.0, 0.0).astype(dtype)


def dot(a, b):
    return lax.dot_general(a, b, (((1,), (0,)), ((), ())), preferred_element_type=jnp.float32)


def flat_parts(start, count, peers, slots, order, flipped=False):
    def peer(n):
        return iota((count, n), 1) == order((iota((count, n), 0) + start) // slots)

    def slot(n):
        return iota((count, n), 1) == (iota((count, n), 0) + start) % slots

    return (slot(slots), peer(peers)) if flipped else (peer(peers), slot(slots))


def straight(block):
    return block


def column(rows_of, lane_of, values):
    picked = dot(onehot(rows_of), values)
    return jnp.sum(jnp.where(lane_of, picked, 0.0), axis=1, keepdims=True)


def index_column(lists, parts):
    high = column(*parts, (lists // 32).astype(jnp.bfloat16))
    low = column(*parts, (lists % 32).astype(jnp.bfloat16))
    return high.astype(jnp.int32) * 32 + low.astype(jnp.int32)


def gather_new_kernel(peers, slots, chunk, points_ref, lists_ref, out_ref, points, lists, picked, in_sems, out_sems):
    total, rows = peers * slots, points.shape[0]
    loads = [pltpu.make_async_copy(lists_ref, lists, in_sems.at[0])]
    for k, start in enumerate(range(0, rows, chunk)):
        part = pl.ds(start, chunk)
        loads.append(pltpu.make_async_copy(points_ref.at[part, :], points.at[part, :], in_sems.at[k + 1]))
    for load in loads:
        load.start()
    loads[0].wait()
    index = index_column(lists[...], flat_parts(0, total, peers, slots, straight, True))
    stores = []
    for c, at in enumerate(range(0, total, chunk)):
        acc = None
        for k, start in enumerate(range(0, rows, chunk)):
            if c == 0:
                loads[k + 1].wait()
            picks = onehot(index[at : at + chunk, :] == iota((chunk, chunk), 1) + start)
            term = dot(picks, points[start : start + chunk, :])
            acc = term if acc is None else acc + term
        picked[at : at + chunk, :] = acc.astype(jnp.bfloat16)
        part = pl.ds(at, chunk)
        stores.append(pltpu.make_async_copy(picked.at[part, :], out_ref.at[part, :], out_sems.at[c]))
        stores[-1].start()
    for store in stores:
        store.wait()


def gather_new(points, lists, peers, slots):
    total, chunk = peers * slots, 256
    rows, features = points.shape
    hbm = pl.BlockSpec(memory_space=pltpu.HBM)
    return pl.pallas_call(
        functools.partial(gather_new_kernel, peers, slots, chunk),
        in_specs=[hbm, hbm],
        out_specs=hbm,
        out_shape=pltpu.HBM((total, features), jnp.bfloat16),
        scratch_shapes=[
            pltpu.VMEM((rows, features), jnp.bfloat16),
            pltpu.VMEM(lists.shape, jnp.int32),
            pltpu.VMEM((total, features), jnp.bfloat16),
            pltpu.SemaphoreType.DMA((rows // chunk + 1,)),
            pltpu.SemaphoreType.DMA((total // chunk,)),
        ],
        compiler_params=pltpu.CompilerParams(vmem_limit_bytes=VMEM_LIMIT),
        cost_estimate=pl.CostEstimate(
            flops=2 * total * rows * features, bytes_accessed=2 * (total + rows) * features, transcendentals=0
        ),
    )(pltpu.with_memory_space_constraint(points, pltpu.HBM), pltpu.with_memory_space_constraint(lists, pltpu.HBM))


def gather_old_kernel(groups, slots, chunk, points_ref, lists_ref, place_ref, *outs):
    rows = points_ref.shape[0]
    size = outs[0].shape[0]
    for start in range(0, groups * slots, chunk):
        parts = flat_parts(start, chunk, groups, slots, lambda block: block ^ place_ref[0])
        index = index_column(lists_ref[...], parts)
        picked = dot(onehot(index == iota((chunk, rows), 1)), points_ref[...]).astype(jnp.bfloat16)
        for at in range(0, chunk, size):
            outs[(start + at) // size][...] = picked[at : at + size, :]


def gather_old(points, lists, place, groups, slots, pieces):
    total = groups * slots
    rows, features = points.shape
    vmem = pl.BlockSpec(memory_space=pltpu.VMEM)
    return pl.pallas_call(
        functools.partial(gather_old_kernel, groups, slots, 256),
        in_specs=[vmem, vmem, pl.BlockSpec(memory_space=pltpu.SMEM)],
        out_shape=(jax.ShapeDtypeStruct((total // pieces, features), jnp.bfloat16),) * pieces,
        compiler_params=pltpu.CompilerParams(vmem_limit_bytes=VMEM_LIMIT),
        cost_estimate=pl.CostEstimate(
            flops=2 * total * rows * features, bytes_accessed=2 * (total + rows) * features, transcendentals=0
        ),
    )(points, lists, place)


def exchange(values, low, high):
    a, b = values[low], values[high]
    values[low], values[high] = jnp.minimum(a, b), jnp.maximum(a, b)


def sort16(values):
    values = list(values)
    for low, high in SORT16:
        exchange(values, low, high)
    return values


def merge16(first, second):
    values = [jnp.minimum(first[k], second[15 - k]) for k in range(16)]
    for gap in (8, 4, 2, 1):
        for k in range(16):
            if not k & gap:
                exchange(values, k, k + gap)
    return values


def block16(ref, start, lanes):
    return [ref[pl.ds(start + SUBLANES * k, SUBLANES), lanes] for k in range(16)]


def smallest16(ref, lanes, held):
    step = 16 * SUBLANES
    first = 0
    if held is None:
        held, first = sort16(block16(ref, 0, lanes)), 1

    def body(t, held):
        start = pl.multiple_of(t * step, step)
        return tuple(merge16(held, sort16(block16(ref, start, lanes))))

    return list(lax.fori_loop(first, ref.shape[0] // step, body, tuple(held)))


def distances(cand, points_ref, own_sq_ref):
    wide = cand.astype(jnp.float32)
    cand_sq = jnp.sum(wide * wide, axis=1, keepdims=True)
    inner = lax.dot_general(
        cand, points_ref[...], (((1,), (1,)), ((), ())), preferred_element_type=jnp.float32
    )
    return cand_sq + own_sq_ref[...] - 2.0 * inner


def usable_slots(counts_ref, start, chunk, peers, slots, order):
    peer_of, _ = flat_parts(start, chunk, peers, slots, order)
    count = jnp.sum(jnp.where(peer_of, counts_ref[...], 0), axis=1, keepdims=True)
    return (iota((chunk, 1), 0) + start) % slots < count


def slot_rows(minima, slots):
    chunk = minima.shape[0]
    spread = jnp.where(iota((chunk, slots), 1) == iota((chunk, slots), 0) % slots, minima, 0.0)
    return [jnp.sum(spread[at : at + slots, :], axis=0, keepdims=True) for at in range(0, chunk, slots)]


def halves_kernel(slots, order, *refs):
    pieces, (mine_ref, handed_ref) = refs[:-2], refs[-2:]
    for k, piece in zip(order, pieces):
        mine_ref[k * slots : (k + 1) * slots, :] = piece[:slots, :]
        handed_ref[k * slots : (k + 1) * slots, :] = piece[slots:, :]


def source_of(count, place_ref):
    return lambda block: jnp.where(block < count, 2 * block, 2 * (block - count) + 1) ^ place_ref[0]


def least_distances(cand, points_ref, own_sq_ref):
    wide = cand.astype(jnp.float32)
    cand_sq = jnp.sum(wide * wide, axis=1, keepdims=True)
    least = None
    for start in range(0, points_ref.shape[0], 256):
        inner = lax.dot_general(
            cand, points_ref[start : start + 256, :], (((1,), (1,)), ((), ())), preferred_element_type=jnp.float32
        )
        for at in range(0, 256, LANES):
            own = own_sq_ref[:, start + at : start + at + LANES]
            dist = cand_sq + own - 2.0 * inner[:, at : at + LANES]
            least = dist if least is None else jnp.minimum(least, dist)
    return jnp.min(least, axis=1, keepdims=True)


def minima_old_kernel(groups, slots, even_ref, odd_ref, points_ref, own_sq_ref, counts_ref, place_ref, minima_ref):
    half = groups // 2 * slots
    order = source_of(groups // 2, place_ref)
    for start, cand_ref in ((0, even_ref), (half, odd_ref)):
        usable = usable_slots(counts_ref, start, half, groups, slots, order)
        minima = jnp.where(usable, least_distances(cand_ref[...], points_ref, own_sq_ref), cap_value)
        for k, row in enumerate(slot_rows(minima, slots)):
            minima_ref[order(start // slots + k)] = row.astype(jnp.bfloat16)


def held_kernel(groups, slots, even_ref, odd_ref, points_ref, own_sq_ref, counts_ref, place_ref, held_ref, dist_ref):
    half = groups // 2 * slots
    order = source_of(groups // 2, place_ref)
    for start, cand_ref in ((0, even_ref), (half, odd_ref)):
        usable = usable_slots(counts_ref, start, half, groups, slots, order)
        dist = distances(cand_ref[...], points_ref, own_sq_ref)
        dist_ref[start : start + half, :] = jnp.where(usable, dist, far_value)

    def block(t, _):
        lanes = pl.ds(pl.multiple_of(t * LANES, LANES), LANES)
        for k, value in enumerate(smallest16(dist_ref, lanes, None)):
            held_ref[SUBLANES * k : SUBLANES * (k + 1), lanes] = value
        return 0

    lax.fori_loop(0, dist_ref.shape[1] // LANES, block, 0)


def minima_kernel(peers, slots, cand_ref, points_ref, own_sq_ref, counts_ref, minima_ref):
    usable = usable_slots(counts_ref, 0, peers * slots, peers, slots, straight)
    minima = jnp.where(usable, least_distances(cand_ref[...], points_ref, own_sq_ref), cap_value)
    for k, row in enumerate(slot_rows(minima, slots)):
        minima_ref[k] = row.astype(jnp.bfloat16)


def select_kernel(
    peers, slots, chunk, cand_ref, points_ref, own_sq_ref, counts_ref, held_hbm_ref, out_ref, dist_ref, held_ref, sem
):
    fetch = pltpu.make_async_copy(held_hbm_ref, held_ref, sem)
    fetch.start()
    for start in range(0, peers * slots, chunk):
        usable = usable_slots(counts_ref, start, chunk, peers, slots, straight)
        dist = distances(cand_ref[start : start + chunk, :], points_ref, own_sq_ref)
        dist_ref[start : start + chunk, :] = jnp.where(usable, dist, far_value)
    fetch.wait()
    sublane = iota((SUBLANES, LANES), 0)

    def block(t, _):
        lanes = pl.ds(pl.multiple_of(t * LANES, LANES), LANES)
        held = smallest16(dist_ref, lanes, block16(held_ref, 0, lanes))
        for shift in (4, 2, 1):
            held = merge16(held, [pltpu.roll(value, shift, 0) for value in held])
        for half in range(2):
            rows = held[SUBLANES * half]
            for k in range(1, SUBLANES):
                rows = jnp.where(sublane == k, held[SUBLANES * half + k], rows)
            out_ref[SUBLANES * half : SUBLANES * (half + 1), lanes] = rows
        return 0

    lax.fori_loop(0, dist_ref.shape[1] // LANES, block, 0)


def ready_kernel(old_lists_ref, old_back_ref, new_lists_ref, best_ref, wide_ref):
    best = jnp.full(best_ref.shape, cap_value, jnp.float32)
    old_back = old_back_ref[...].reshape(old_lists_ref.shape).astype(jnp.float32)
    peers, slots = old_lists_ref.shape
    for c in range(slots):
        for at in range(0, peers, SUBLANES):
            index = old_lists_ref[at : at + SUBLANES, c : c + 1]
            value = old_back[at : at + SUBLANES, c : c + 1]
            best = jnp.where(index == iota(best.shape, 1), jnp.minimum(best, value), best)
    best_ref[...] = best
    peers, slots = new_lists_ref.shape
    for c in range(slots):
        wide_ref[c * peers : (c + 1) * peers, :] = jnp.broadcast_to(new_lists_ref[:, c : c + 1], (peers, LANES))


def reverse_kernel(back_ref, best_ref, wide_ref, out_ref):
    peers, _, slots = back_ref.shape
    back = back_ref[...].reshape(peers, slots).astype(jnp.float32)
    lane = iota((SUBLANES, LANES), 1)
    best = [best_ref[:, LANES * k : LANES * (k + 1)] for k in range(SUBLANES)]
    for c in range(slots):
        for at in range(0, peers, SUBLANES):
            index = wide_ref[c * peers + at : c * peers + at + SUBLANES, :]
            value = back[at : at + SUBLANES, c : c + 1]
            for k in range(SUBLANES):
                best[k] = jnp.minimum(best[k], jnp.where(index == lane + k * LANES, value, cap_value))
    for k in range(SUBLANES):
        out_ref[k : k + 1, :] = jnp.min(best[k], axis=0, keepdims=True)


def apart(groups, away):
    return [(g, g ^ away) for g in range(groups)]


def body(points, serve_new, serve_old, count_new, count_old):
    rows, features = points.shape
    peers, slots = serve_new.shape
    groups, group_slots = serve_old.shape
    lists_new = serve_new.T
    counts_new, counts_old = count_new.T, count_old.T
    params = pltpu.CompilerParams(vmem_limit_bytes=VMEM_LIMIT)
    vmem = pl.BlockSpec(memory_space=pltpu.VMEM)
    smem = pl.BlockSpec(memory_space=pltpu.SMEM)
    place = lax.axis_index("grp").astype(jnp.int32).reshape(1)

    offered_new = gather_new(points, lists_new, peers, slots)
    pulled_new = lax.all_to_all(
        offered_new.reshape(peers, slots, features), "shard", split_axis=0, concat_axis=0, tiled=True
    ).reshape(peers * slots, features)

    pieces = gather_old(points, serve_old, place, groups, group_slots, groups // 2)
    spread = (4, 2, 6, 3, 7, 5, 1)
    order = tuple(k for k in spread if k < groups // 2) + tuple(range(len(spread) + 1, groups // 2))
    came = [lax.ppermute(pieces[k], "grp", apart(groups, 2 * k)) for k in order]
    half = groups // 2 * group_slots
    evens, handed = pl.pallas_call(
        functools.partial(halves_kernel, group_slots, order + (0,)),
        out_shape=(jax.ShapeDtypeStruct((half, features), jnp.bfloat16),) * 2,
        compiler_params=params,
        cost_estimate=pl.CostEstimate(flops=0, bytes_accessed=8 * half * features, transcendentals=0),
    )(*came, pieces[0])
    odds = lax.ppermute(handed, "grp", apart(groups, 1))

    own_sq = jnp.sum(jnp.square(points.astype(jnp.float32)), axis=1)[None, :]

    total_old = groups * group_slots
    old_cost = pl.CostEstimate(
        flops=2 * total_old * rows * features, bytes_accessed=2 * (total_old + rows) * features, transcendentals=0
    )
    minima_old = pl.pallas_call(
        functools.partial(minima_old_kernel, groups, group_slots),
        in_specs=[vmem] * 5 + [smem],
        out_shape=jax.ShapeDtypeStruct((groups, 1, group_slots), jnp.bfloat16),
        compiler_params=params,
        cost_estimate=old_cost,
    )(evens, odds, points, own_sq, counts_old, place)
    pulled_new, minima_old = lax.optimization_barrier((pulled_new, minima_old))
    back_old = lax.all_to_all(minima_old, "grp", split_axis=0, concat_axis=0, tiled=True)

    total_new = peers * slots
    minima_new = pl.pallas_call(
        functools.partial(minima_kernel, peers, slots),
        out_shape=jax.ShapeDtypeStruct((peers, 1, slots), jnp.bfloat16),
        compiler_params=params,
        cost_estimate=pl.CostEstimate(
            flops=2 * total_new * rows * features, bytes_accessed=4 * total_new * features, transcendentals=0
        ),
    )(pulled_new, points, own_sq, counts_new)
    back_new = lax.all_to_all(minima_new, "shard", split_axis=0, concat_axis=0, tiled=True)

    evens, _ = lax.optimization_barrier((evens, pulled_new))
    held = pl.pallas_call(
        functools.partial(held_kernel, groups, group_slots),
        in_specs=[vmem] * 5 + [smem],
        out_shape=pltpu.HBM((16 * SUBLANES, rows), jnp.float32),
        scratch_shapes=[pltpu.VMEM((total_old, rows), jnp.float32)],
        compiler_params=params,
        cost_estimate=old_cost,
    )(evens, odds, points, own_sq, counts_old, place)
    pulled_new, back_old, _ = lax.optimization_barrier((pulled_new, back_old, minima_new))
    nearest = pl.pallas_call(
        functools.partial(select_kernel, peers, slots, 256),
        in_specs=[vmem] * 4 + [pl.BlockSpec(memory_space=pltpu.HBM)],
        out_shape=jax.ShapeDtypeStruct((NEAR, rows), jnp.float32),
        scratch_shapes=[
            pltpu.VMEM((total_new, rows), jnp.float32),
            pltpu.VMEM((16 * SUBLANES, rows), jnp.float32),
            pltpu.SemaphoreType.DMA,
        ],
        compiler_params=params,
        cost_estimate=pl.CostEstimate(
            flops=4 * total_new * rows * features, bytes_accessed=4 * total_new * features, transcendentals=0
        ),
    )(pulled_new, points, own_sq, counts_new, pltpu.with_memory_space_constraint(held, pltpu.HBM))

    nearest, back_old = lax.optimization_barrier((nearest, back_old))
    best, wide = pl.pallas_call(
        ready_kernel,
        out_shape=(
            jax.ShapeDtypeStruct((SUBLANES, rows), jnp.float32),
            jax.ShapeDtypeStruct((total_new, LANES), jnp.int32),
        ),
        compiler_params=params,
    )(serve_old, back_old, serve_new)
    reverse = pl.pallas_call(
        reverse_kernel,
        out_shape=jax.ShapeDtypeStruct((SUBLANES, LANES), jnp.float32),
        compiler_params=params,
    )(back_new, best, wide)
    return nearest.T, reverse.reshape(rows)


def solution(mesh):
    placed = (P(("grp", "shard"), None),) * 5
    return jax.shard_map(
        body,
        mesh=mesh,
        in_specs=placed,
        out_specs=(P(("grp", "shard"), None), P(("grp", "shard"))),
        check_vma=False,
    )
```

```python
import functools

import jax
import jax.numpy as jnp
from jax import lax
from jax.experimental import pallas as pl
from jax.experimental.pallas import tpu as pltpu
from jax.sharding import PartitionSpec as P

NEAR = 16
LANES = 128
SUBLANES = 8

cap_value = 8.0
far_value = 1000000000.0

VMEM_LIMIT = 20 * 1024 * 1024

SORT16 = (
    (0, 13), (1, 12), (2, 15), (3, 14), (4, 8), (5, 6), (7, 11), (9, 10),
    (0, 5), (1, 7), (2, 9), (3, 4), (6, 13), (8, 14), (10, 15), (11, 12),
    (0, 1), (2, 3), (4, 5), (6, 8), (7, 9), (10, 11), (12, 13), (14, 15),
    (0, 2), (1, 3), (4, 10), (5, 11), (6, 7), (8, 9), (12, 14), (13, 15),
    (1, 2), (3, 12), (4, 6), (5, 7), (8, 10), (9, 11), (13, 14),
    (1, 4), (2, 6), (5, 8), (7, 10), (9, 13), (11, 14),
    (2, 4), (3, 6), (9, 12), (11, 13),
    (3, 5), (6, 8), (7, 9), (10, 12),
    (3, 4), (5, 6), (7, 8), (9, 10), (11, 12),
    (6, 7), (8, 9),
)


def iota(shape, dim):
    return lax.broadcasted_iota(jnp.int32, shape, dim)


def onehot(condition, dtype=jnp.bfloat16):
    return jnp.where(condition, 1.0, 0.0).astype(dtype)


def dot(a, b):
    return lax.dot_general(a, b, (((1,), (0,)), ((), ())), preferred_element_type=jnp.float32)


def flat_parts(start, count, peers, slots, order, flipped=False):
    def peer(n):
        return iota((count, n), 1) == order((iota((count, n), 0) + start) // slots)

    def slot(n):
        return iota((count, n), 1) == (iota((count, n), 0) + start) % slots

    return (slot(slots), peer(peers)) if flipped else (peer(peers), slot(slots))


def straight(block):
    return block


def column(rows_of, lane_of, values):
    picked = dot(onehot(rows_of), values)
    return jnp.sum(jnp.where(lane_of, picked, 0.0), axis=1, keepdims=True)


def index_column(lists, parts):
    high = column(*parts, (lists // 32).astype(jnp.bfloat16))
    low = column(*parts, (lists % 32).astype(jnp.bfloat16))
    return high.astype(jnp.int32) * 32 + low.astype(jnp.int32)


def gather_new_kernel(peers, slots, chunk, points_ref, lists_ref, out_ref, points, lists, picked, in_sems, out_sems):
    total, rows = peers * slots, points.shape[0]
    loads = [pltpu.make_async_copy(lists_ref, lists, in_sems.at[0])]
    for k, start in enumerate(range(0, rows, chunk)):
        part = pl.ds(start, chunk)
        loads.append(pltpu.make_async_copy(points_ref.at[part, :], points.at[part, :], in_sems.at[k + 1]))
    for load in loads:
        load.start()
    loads[0].wait()
    index = index_column(lists[...], flat_parts(0, total, peers, slots, straight, True))
    stores = []
    for c, at in enumerate(range(0, total, chunk)):
        acc = None
        for k, start in enumerate(range(0, rows, chunk)):
            if c == 0:
                loads[k + 1].wait()
            picks = onehot(index[at : at + chunk, :] == iota((chunk, chunk), 1) + start)
            term = dot(picks, points[start : start + chunk, :])
            acc = term if acc is None else acc + term
        picked[at : at + chunk, :] = acc.astype(jnp.bfloat16)
        part = pl.ds(at, chunk)
        stores.append(pltpu.make_async_copy(picked.at[part, :], out_ref.at[part, :], out_sems.at[c]))
        stores[-1].start()
    for store in stores:
        store.wait()


def gather_new(points, lists, peers, slots):
    total, chunk = peers * slots, 256
    rows, features = points.shape
    hbm = pl.BlockSpec(memory_space=pltpu.HBM)
    return pl.pallas_call(
        functools.partial(gather_new_kernel, peers, slots, chunk),
        in_specs=[hbm, hbm],
        out_specs=hbm,
        out_shape=pltpu.HBM((total, features), jnp.bfloat16),
        scratch_shapes=[
            pltpu.VMEM((rows, features), jnp.bfloat16),
            pltpu.VMEM(lists.shape, jnp.int32),
            pltpu.VMEM((total, features), jnp.bfloat16),
            pltpu.SemaphoreType.DMA((rows // chunk + 1,)),
            pltpu.SemaphoreType.DMA((total // chunk,)),
        ],
        compiler_params=pltpu.CompilerParams(vmem_limit_bytes=VMEM_LIMIT),
        cost_estimate=pl.CostEstimate(
            flops=2 * total * rows * features, bytes_accessed=2 * (total + rows) * features, transcendentals=0
        ),
    )(pltpu.with_memory_space_constraint(points, pltpu.HBM), pltpu.with_memory_space_constraint(lists, pltpu.HBM))


def gather_old_kernel(groups, slots, chunk, points_ref, lists_ref, place_ref, *outs):
    rows = points_ref.shape[0]
    size = outs[0].shape[0]
    for start in range(0, groups * slots, chunk):
        parts = flat_parts(start, chunk, groups, slots, lambda block: block ^ place_ref[0])
        index = index_column(lists_ref[...], parts)
        picked = dot(onehot(index == iota((chunk, rows), 1)), points_ref[...]).astype(jnp.bfloat16)
        for at in range(0, chunk, size):
            outs[(start + at) // size][...] = picked[at : at + size, :]


def gather_old(points, lists, place, groups, slots, pieces):
    total = groups * slots
    rows, features = points.shape
    vmem = pl.BlockSpec(memory_space=pltpu.VMEM)
    return pl.pallas_call(
        functools.partial(gather_old_kernel, groups, slots, 256),
        in_specs=[vmem, vmem, pl.BlockSpec(memory_space=pltpu.SMEM)],
        out_shape=(jax.ShapeDtypeStruct((total // pieces, features), jnp.bfloat16),) * pieces,
        compiler_params=pltpu.CompilerParams(vmem_limit_bytes=VMEM_LIMIT),
        cost_estimate=pl.CostEstimate(
            flops=2 * total * rows * features, bytes_accessed=2 * (total + rows) * features, transcendentals=0
        ),
    )(points, lists, place)


def exchange(values, low, high):
    a, b = values[low], values[high]
    values[low], values[high] = jnp.minimum(a, b), jnp.maximum(a, b)


def sort16(values):
    values = list(values)
    for low, high in SORT16:
        exchange(values, low, high)
    return values


def merge16(first, second):
    values = [jnp.minimum(first[k], second[15 - k]) for k in range(16)]
    for gap in (8, 4, 2, 1):
        for k in range(16):
            if not k & gap:
                exchange(values, k, k + gap)
    return values


def block16(ref, start, lanes):
    return [ref[pl.ds(start + SUBLANES * k, SUBLANES), lanes] for k in range(16)]


def smallest16(ref, lanes, held):
    step = 16 * SUBLANES
    first = 0
    if held is None:
        held, first = sort16(block16(ref, 0, lanes)), 1

    def body(t, held):
        start = pl.multiple_of(t * step, step)
        return tuple(merge16(held, sort16(block16(ref, start, lanes))))

    return list(lax.fori_loop(first, ref.shape[0] // step, body, tuple(held)))


def distances(cand, points_ref, own_sq_ref):
    wide = cand.astype(jnp.float32)
    cand_sq = jnp.sum(wide * wide, axis=1, keepdims=True)
    inner = lax.dot_general(
        cand, points_ref[...], (((1,), (1,)), ((), ())), preferred_element_type=jnp.float32
    )
    return cand_sq + own_sq_ref[...] - 2.0 * inner


def usable_slots(counts_ref, start, chunk, peers, slots, order):
    peer_of, _ = flat_parts(start, chunk, peers, slots, order)
    count = jnp.sum(jnp.where(peer_of, counts_ref[...], 0), axis=1, keepdims=True)
    return (iota((chunk, 1), 0) + start) % slots < count


def slot_rows(minima, slots):
    chunk = minima.shape[0]
    spread = jnp.where(iota((chunk, slots), 1) == iota((chunk, slots), 0) % slots, minima, 0.0)
    return [jnp.sum(spread[at : at + slots, :], axis=0, keepdims=True) for at in range(0, chunk, slots)]


def halves_kernel(slots, order, *refs):
    pieces, (mine_ref, handed_ref) = refs[:-2], refs[-2:]
    for k, piece in zip(order, pieces):
        mine_ref[k * slots : (k + 1) * slots, :] = piece[:slots, :]
        handed_ref[k * slots : (k + 1) * slots, :] = piece[slots:, :]


def source_of(count, place_ref):
    return lambda block: jnp.where(block < count, 2 * block, 2 * (block - count) + 1) ^ place_ref[0]


def least_distances(cand, points_ref, own_sq_ref):
    wide = cand.astype(jnp.float32)
    cand_sq = jnp.sum(wide * wide, axis=1, keepdims=True)
    least = None
    for start in range(0, points_ref.shape[0], 256):
        inner = lax.dot_general(
            cand, points_ref[start : start + 256, :], (((1,), (1,)), ((), ())), preferred_element_type=jnp.float32
        )
        for at in range(0, 256, LANES):
            own = own_sq_ref[:, start + at : start + at + LANES]
            dist = cand_sq + own - 2.0 * inner[:, at : at + LANES]
            least = dist if least is None else jnp.minimum(least, dist)
    return jnp.min(least, axis=1, keepdims=True)


def hold(dist_ref, before_ref, held_ref):
    def block(t, _):
        lanes = pl.ds(pl.multiple_of(t * LANES, LANES), LANES)
        before = None if before_ref is None else block16(before_ref, 0, lanes)
        for k, value in enumerate(smallest16(dist_ref, lanes, before)):
            held_ref[SUBLANES * k : SUBLANES * (k + 1), lanes] = value
        return 0

    lax.fori_loop(0, dist_ref.shape[1] // LANES, block, 0)


def even_kernel(groups, slots, cand_ref, points_ref, own_sq_ref, counts_ref, place_ref, rows_ref, held_ref, dist_ref):
    half = groups // 2 * slots
    usable = usable_slots(counts_ref, 0, half, groups, slots, source_of(groups // 2, place_ref))
    dist = distances(cand_ref[...], points_ref, own_sq_ref)
    dist_ref[...] = jnp.where(usable, dist, far_value)
    minima = jnp.where(usable, jnp.min(dist, axis=1, keepdims=True), cap_value)
    for k, row in enumerate(slot_rows(minima, slots)):
        rows_ref[k : k + 1, :] = row
    hold(dist_ref, None, held_ref)


def minima_old_kernel(groups, slots, cand_ref, points_ref, own_sq_ref, counts_ref, rows_ref, place_ref, minima_ref):
    count = groups // 2
    order = source_of(count, place_ref)
    usable = usable_slots(counts_ref, count * slots, count * slots, groups, slots, order)
    minima = jnp.where(usable, least_distances(cand_ref[...], points_ref, own_sq_ref), cap_value)
    for k, row in enumerate(slot_rows(minima, slots)):
        minima_ref[order(k)] = rows_ref[k : k + 1, :].astype(jnp.bfloat16)
        minima_ref[order(count + k)] = row.astype(jnp.bfloat16)


def odd_kernel(
    groups, slots, cand_ref, points_ref, own_sq_ref, counts_ref, place_ref, before_hbm_ref, held_ref,
    dist_ref, before_ref, sem,
):
    fetch = pltpu.make_async_copy(before_hbm_ref, before_ref, sem)
    fetch.start()
    half = groups // 2 * slots
    usable = usable_slots(counts_ref, half, half, groups, slots, source_of(groups // 2, place_ref))
    dist_ref[...] = jnp.where(usable, distances(cand_ref[...], points_ref, own_sq_ref), far_value)
    fetch.wait()
    hold(dist_ref, before_ref, held_ref)


def minima_kernel(peers, slots, cand_ref, points_ref, own_sq_ref, counts_ref, minima_ref):
    usable = usable_slots(counts_ref, 0, peers * slots, peers, slots, straight)
    minima = jnp.where(usable, least_distances(cand_ref[...], points_ref, own_sq_ref), cap_value)
    for k, row in enumerate(slot_rows(minima, slots)):
        minima_ref[k] = row.astype(jnp.bfloat16)


def select_kernel(
    peers, slots, chunk, cand_ref, points_ref, own_sq_ref, counts_ref, held_hbm_ref, out_ref, dist_ref, held_ref, sem
):
    fetch = pltpu.make_async_copy(held_hbm_ref, held_ref, sem)
    fetch.start()
    for start in range(0, peers * slots, chunk):
        usable = usable_slots(counts_ref, start, chunk, peers, slots, straight)
        dist = distances(cand_ref[start : start + chunk, :], points_ref, own_sq_ref)
        dist_ref[start : start + chunk, :] = jnp.where(usable, dist, far_value)
    fetch.wait()
    sublane = iota((SUBLANES, LANES), 0)

    def block(t, _):
        lanes = pl.ds(pl.multiple_of(t * LANES, LANES), LANES)
        held = smallest16(dist_ref, lanes, block16(held_ref, 0, lanes))
        for shift in (4, 2, 1):
            held = merge16(held, [pltpu.roll(value, shift, 0) for value in held])
        for half in range(2):
            rows = held[SUBLANES * half]
            for k in range(1, SUBLANES):
                rows = jnp.where(sublane == k, held[SUBLANES * half + k], rows)
            out_ref[SUBLANES * half : SUBLANES * (half + 1), lanes] = rows
        return 0

    lax.fori_loop(0, dist_ref.shape[1] // LANES, block, 0)


def ready_kernel(old_lists_ref, old_back_ref, new_lists_ref, best_ref, wide_ref):
    best = jnp.full(best_ref.shape, cap_value, jnp.float32)
    old_back = old_back_ref[...].reshape(old_lists_ref.shape).astype(jnp.float32)
    peers, slots = old_lists_ref.shape
    for c in range(slots):
        for at in range(0, peers, SUBLANES):
            index = old_lists_ref[at : at + SUBLANES, c : c + 1]
            value = old_back[at : at + SUBLANES, c : c + 1]
            best = jnp.where(index == iota(best.shape, 1), jnp.minimum(best, value), best)
    best_ref[...] = best
    slots, peers = new_lists_ref.shape
    same = onehot(iota((slots, slots), 0) == iota((slots, slots), 1))

    def upright(values):
        return lax.dot_general(
            values.astype(jnp.bfloat16), same, (((0,), (0,)), ((), ())), preferred_element_type=jnp.float32
        ).astype(jnp.int32)

    lists = upright(new_lists_ref[...] // 32) * 32 + upright(new_lists_ref[...] % 32)
    for c in range(slots):
        wide_ref[c * peers : (c + 1) * peers, :] = jnp.broadcast_to(lists[:, c : c + 1], (peers, LANES))


def reverse_kernel(back_ref, best_ref, wide_ref, out_ref):
    peers, _, slots = back_ref.shape
    back = back_ref[...].reshape(peers, slots).astype(jnp.float32)
    lane = iota((SUBLANES, LANES), 1)
    best = [best_ref[:, LANES * k : LANES * (k + 1)] for k in range(SUBLANES)]
    for c in range(slots):
        for at in range(0, peers, SUBLANES):
            index = wide_ref[c * peers + at : c * peers + at + SUBLANES, :]
            value = back[at : at + SUBLANES, c : c + 1]
            for k in range(SUBLANES):
                best[k] = jnp.minimum(best[k], jnp.where(index == lane + k * LANES, value, cap_value))
    for k in range(SUBLANES):
        out_ref[k : k + 1, :] = jnp.min(best[k], axis=0, keepdims=True)


def apart(groups, away):
    return [(g, g ^ away) for g in range(groups)]


def body(points, serve_new, serve_old, count_new, count_old):
    rows, features = points.shape
    peers, slots = serve_new.shape
    groups, group_slots = serve_old.shape
    lists_new = serve_new.T
    counts_new, counts_old = count_new.T, count_old.T
    params = pltpu.CompilerParams(vmem_limit_bytes=VMEM_LIMIT)
    vmem = pl.BlockSpec(memory_space=pltpu.VMEM)
    smem = pl.BlockSpec(memory_space=pltpu.SMEM)
    place = lax.axis_index("grp").astype(jnp.int32).reshape(1)

    offered_new = gather_new(points, lists_new, peers, slots)
    pulled_new = lax.all_to_all(
        offered_new.reshape(peers, slots, features), "shard", split_axis=0, concat_axis=0, tiled=True
    ).reshape(peers * slots, features)

    pieces = gather_old(points, serve_old, place, groups, group_slots, groups // 2)
    spread = (4, 2, 6, 3, 7, 5, 1)
    order = tuple(k for k in spread if k < groups // 2) + tuple(range(len(spread) + 1, groups // 2))
    came = [lax.ppermute(pieces[k], "grp", apart(groups, 2 * k)) for k in order]
    own_sq = jnp.sum(jnp.square(points.astype(jnp.float32)), axis=1)[None, :]
    own_sq, own_piece = lax.optimization_barrier((own_sq, pieces[0]))

    half = groups // 2 * group_slots
    evens, handed = pl.pallas_call(
        functools.partial(halves_kernel, group_slots, order + (0,)),
        out_shape=(jax.ShapeDtypeStruct((half, features), jnp.bfloat16),) * 2,
        compiler_params=params,
        cost_estimate=pl.CostEstimate(flops=0, bytes_accessed=8 * half * features, transcendentals=0),
    )(*came, own_piece)
    odds = lax.ppermute(handed, "grp", apart(groups, 1))

    old_cost = pl.CostEstimate(
        flops=2 * half * rows * features, bytes_accessed=2 * (half + rows) * features, transcendentals=0
    )
    held_shape = (16 * SUBLANES, rows)
    minima_even, held = pl.pallas_call(
        functools.partial(even_kernel, groups, group_slots),
        in_specs=[vmem] * 4 + [smem],
        out_shape=(
            jax.ShapeDtypeStruct((groups // 2, group_slots), jnp.float32),
            pltpu.HBM(held_shape, jnp.float32),
        ),
        scratch_shapes=[pltpu.VMEM((half, rows), jnp.float32)],
        compiler_params=params,
        cost_estimate=old_cost,
    )(evens, points, own_sq, counts_old, place)
    minima_old = pl.pallas_call(
        functools.partial(minima_old_kernel, groups, group_slots),
        in_specs=[vmem] * 5 + [smem],
        out_shape=jax.ShapeDtypeStruct((groups, 1, group_slots), jnp.bfloat16),
        compiler_params=params,
        cost_estimate=old_cost,
    )(odds, points, own_sq, counts_old, minima_even, place)

    pulled_new, minima_old = lax.optimization_barrier((pulled_new, minima_old))
    back_old = lax.all_to_all(minima_old, "grp", split_axis=0, concat_axis=0, tiled=True)

    total_new = peers * slots
    minima_new = pl.pallas_call(
        functools.partial(minima_kernel, peers, slots),
        out_shape=jax.ShapeDtypeStruct((peers, 1, slots), jnp.bfloat16),
        compiler_params=params,
        cost_estimate=pl.CostEstimate(
            flops=2 * total_new * rows * features, bytes_accessed=4 * total_new * features, transcendentals=0
        ),
    )(pulled_new, points, own_sq, counts_new)
    back_new = lax.all_to_all(minima_new, "shard", split_axis=0, concat_axis=0, tiled=True)

    odds, _ = lax.optimization_barrier((odds, pulled_new))
    hbm = pl.BlockSpec(memory_space=pltpu.HBM)
    held = pl.pallas_call(
        functools.partial(odd_kernel, groups, group_slots),
        in_specs=[vmem] * 4 + [smem, hbm],
        out_shape=pltpu.HBM(held_shape, jnp.float32),
        scratch_shapes=[
            pltpu.VMEM((half, rows), jnp.float32),
            pltpu.VMEM(held_shape, jnp.float32),
            pltpu.SemaphoreType.DMA,
        ],
        compiler_params=params,
        cost_estimate=old_cost,
    )(odds, points, own_sq, counts_old, place, pltpu.with_memory_space_constraint(held, pltpu.HBM))
    pulled_new, back_old, _ = lax.optimization_barrier((pulled_new, back_old, minima_new))
    nearest = pl.pallas_call(
        functools.partial(select_kernel, peers, slots, 256),
        in_specs=[vmem] * 4 + [hbm],
        out_shape=jax.ShapeDtypeStruct((NEAR, rows), jnp.float32),
        scratch_shapes=[
            pltpu.VMEM((total_new, rows), jnp.float32),
            pltpu.VMEM(held_shape, jnp.float32),
            pltpu.SemaphoreType.DMA,
        ],
        compiler_params=params,
        cost_estimate=pl.CostEstimate(
            flops=4 * total_new * rows * features, bytes_accessed=4 * total_new * features, transcendentals=0
        ),
    )(pulled_new, points, own_sq, counts_new, pltpu.with_memory_space_constraint(held, pltpu.HBM))

    nearest, back_old = lax.optimization_barrier((nearest, back_old))
    best, wide = pl.pallas_call(
        ready_kernel,
        out_shape=(
            jax.ShapeDtypeStruct((SUBLANES, rows), jnp.float32),
            jax.ShapeDtypeStruct((total_new, LANES), jnp.int32),
        ),
        compiler_params=params,
    )(serve_old, back_old, lists_new)
    reverse = pl.pallas_call(
        reverse_kernel,
        out_shape=jax.ShapeDtypeStruct((SUBLANES, LANES), jnp.float32),
        compiler_params=params,
    )(back_new, best, wide)
    return nearest.T, reverse.reshape(rows)


def solution(mesh):
    placed = (P(("grp", "shard"), None),) * 5
    return jax.shard_map(
        body,
        mesh=mesh,
        in_specs=placed,
        out_specs=(P(("grp", "shard"), None), P(("grp", "shard"))),
        check_vma=False,
    )
```

```python
import functools

import jax
import jax.numpy as jnp
from jax import lax
from jax.experimental import pallas as pl
from jax.experimental.pallas import tpu as pltpu
from jax.sharding import PartitionSpec as P

NEAR = 16
LANES = 128
SUBLANES = 8

cap_value = 8.0
far_value = 1000000000.0

VMEM_LIMIT = 20 * 1024 * 1024

SORT16 = (
    (0, 13), (1, 12), (2, 15), (3, 14), (4, 8), (5, 6), (7, 11), (9, 10),
    (0, 5), (1, 7), (2, 9), (3, 4), (6, 13), (8, 14), (10, 15), (11, 12),
    (0, 1), (2, 3), (4, 5), (6, 8), (7, 9), (10, 11), (12, 13), (14, 15),
    (0, 2), (1, 3), (4, 10), (5, 11), (6, 7), (8, 9), (12, 14), (13, 15),
    (1, 2), (3, 12), (4, 6), (5, 7), (8, 10), (9, 11), (13, 14),
    (1, 4), (2, 6), (5, 8), (7, 10), (9, 13), (11, 14),
    (2, 4), (3, 6), (9, 12), (11, 13),
    (3, 5), (6, 8), (7, 9), (10, 12),
    (3, 4), (5, 6), (7, 8), (9, 10), (11, 12),
    (6, 7), (8, 9),
)


def iota(shape, dim):
    return lax.broadcasted_iota(jnp.int32, shape, dim)


def onehot(condition, dtype=jnp.bfloat16):
    return jnp.where(condition, 1.0, 0.0).astype(dtype)


def dot(a, b):
    return lax.dot_general(a, b, (((1,), (0,)), ((), ())), preferred_element_type=jnp.float32)


def flat_parts(start, count, peers, slots, order, flipped=False):
    def peer(n):
        return iota((count, n), 1) == order((iota((count, n), 0) + start) // slots)

    def slot(n):
        return iota((count, n), 1) == (iota((count, n), 0) + start) % slots

    return (slot(slots), peer(peers)) if flipped else (peer(peers), slot(slots))


def straight(block):
    return block


def column(rows_of, lane_of, values):
    picked = dot(onehot(rows_of), values)
    return jnp.sum(jnp.where(lane_of, picked, 0.0), axis=1, keepdims=True)


def index_column(lists, parts):
    rows_of, lane_of = parts
    rows_of = onehot(rows_of)
    high = dot(rows_of, (lists // 32).astype(jnp.bfloat16))
    low = dot(rows_of, (lists % 32).astype(jnp.bfloat16))
    return jnp.sum(jnp.where(lane_of, high * 32.0 + low, 0.0), axis=1, keepdims=True).astype(jnp.int32)


def gather_new_kernel(
    peers, slots, chunk, points_ref, lists_ref, out_ref, points, lists, picked, first, in_sems, out_sems
):
    total, rows = peers * slots, points_ref.shape[0]
    loads = [pltpu.make_async_copy(lists_ref, lists, in_sems.at[0])]
    for k in range(4):
        part = pl.ds(k * (rows // 4), rows // 4)
        loads.append(pltpu.make_async_copy(points_ref.at[part, :], points.at[part, :], in_sems.at[k + 1]))
    for load in loads:
        load.start()
    loads[0].wait()
    index = index_column(lists[...], flat_parts(0, total, peers, slots, straight, True))
    half = rows // 2
    stores = []
    for h in range(2):
        loads[1 + 2 * h].wait()
        loads[2 + 2 * h].wait()
        for c, at in enumerate(range(0, total, chunk)):
            picks = onehot(index[at : at + chunk, :] == iota((chunk, half), 1) + h * half)
            term = dot(picks, points[h * half : (h + 1) * half, :])
            if h == 0:
                first[at : at + chunk, :] = term
                continue
            picked[at : at + chunk, :] = (first[at : at + chunk, :] + term).astype(jnp.bfloat16)
            part = pl.ds(at, chunk)
            stores.append(pltpu.make_async_copy(picked.at[part, :], out_ref.at[part, :], out_sems.at[c]))
            stores[-1].start()
    for store in stores:
        store.wait()


def gather_new(points, lists, peers, slots):
    total, chunk = peers * slots, 128
    rows, features = points.shape
    hbm = pl.BlockSpec(memory_space=pltpu.HBM)
    return pl.pallas_call(
        functools.partial(gather_new_kernel, peers, slots, chunk),
        in_specs=[hbm, hbm],
        out_specs=hbm,
        out_shape=pltpu.HBM((total, features), jnp.bfloat16),
        scratch_shapes=[
            pltpu.VMEM((rows, features), jnp.bfloat16),
            pltpu.VMEM(lists.shape, jnp.int32),
            pltpu.VMEM((total, features), jnp.bfloat16),
            pltpu.VMEM((total, features), jnp.float32),
            pltpu.SemaphoreType.DMA((5,)),
            pltpu.SemaphoreType.DMA((total // chunk,)),
        ],
        compiler_params=pltpu.CompilerParams(vmem_limit_bytes=VMEM_LIMIT),
        cost_estimate=pl.CostEstimate(
            flops=2 * total * rows * features, bytes_accessed=2 * (total + rows) * features, transcendentals=0
        ),
    )(pltpu.with_memory_space_constraint(points, pltpu.HBM), pltpu.with_memory_space_constraint(lists, pltpu.HBM))


def gather_old_kernel(groups, slots, chunk, points_ref, lists_ref, place_ref, *outs):
    rows = points_ref.shape[0]
    size = outs[0].shape[0]
    for start in range(0, groups * slots, chunk):
        parts = flat_parts(start, chunk, groups, slots, lambda block: block ^ place_ref[0])
        index = index_column(lists_ref[...], parts)
        picked = dot(onehot(index == iota((chunk, rows), 1)), points_ref[...]).astype(jnp.bfloat16)
        for at in range(0, chunk, size):
            outs[(start + at) // size][...] = picked[at : at + size, :]


def gather_old(points, lists, place, groups, slots, pieces):
    total = groups * slots
    rows, features = points.shape
    vmem = pl.BlockSpec(memory_space=pltpu.VMEM)
    return pl.pallas_call(
        functools.partial(gather_old_kernel, groups, slots, 256),
        in_specs=[vmem, vmem, pl.BlockSpec(memory_space=pltpu.SMEM)],
        out_shape=(jax.ShapeDtypeStruct((total // pieces, features), jnp.bfloat16),) * pieces,
        compiler_params=pltpu.CompilerParams(vmem_limit_bytes=VMEM_LIMIT),
        cost_estimate=pl.CostEstimate(
            flops=2 * total * rows * features, bytes_accessed=2 * (total + rows) * features, transcendentals=0
        ),
    )(points, lists, place)


def exchange(values, low, high):
    a, b = values[low], values[high]
    values[low], values[high] = jnp.minimum(a, b), jnp.maximum(a, b)


def sort16(values):
    values = list(values)
    for low, high in SORT16:
        exchange(values, low, high)
    return values


def merge16(first, second):
    values = [jnp.minimum(first[k], second[15 - k]) for k in range(16)]
    for gap in (8, 4, 2, 1):
        for k in range(16):
            if not k & gap:
                exchange(values, k, k + gap)
    return values


def block16(ref, start, lanes):
    return [ref[pl.ds(start + SUBLANES * k, SUBLANES), lanes] for k in range(16)]


def smallest16(ref, lanes, held):
    step = 16 * SUBLANES
    first = 0
    if held is None:
        held, first = sort16(block16(ref, 0, lanes)), 1

    def body(t, held):
        start = pl.multiple_of(t * step, step)
        return tuple(merge16(held, sort16(block16(ref, start, lanes))))

    return list(lax.fori_loop(first, ref.shape[0] // step, body, tuple(held)))


def distances(cand, points_ref, own_sq_ref):
    wide = cand.astype(jnp.float32)
    cand_sq = jnp.sum(wide * wide, axis=1, keepdims=True)
    inner = lax.dot_general(
        cand, points_ref[...], (((1,), (1,)), ((), ())), preferred_element_type=jnp.float32
    )
    return cand_sq + own_sq_ref[...] - 2.0 * inner


def usable_slots(counts_ref, start, chunk, peers, slots, order):
    peer_of, _ = flat_parts(start, chunk, peers, slots, order)
    count = jnp.sum(jnp.where(peer_of, counts_ref[...], 0), axis=1, keepdims=True)
    return (iota((chunk, 1), 0) + start) % slots < count


def slot_rows(minima, slots):
    chunk = minima.shape[0]
    spread = jnp.where(iota((chunk, slots), 1) == iota((chunk, slots), 0) % slots, minima, 0.0)
    return [jnp.sum(spread[at : at + slots, :], axis=0, keepdims=True) for at in range(0, chunk, slots)]


def halves_kernel(slots, order, *refs):
    pieces, (mine_ref, handed_ref) = refs[:-2], refs[-2:]
    for k, piece in zip(order, pieces):
        mine_ref[k * slots : (k + 1) * slots, :] = piece[:slots, :]
        handed_ref[k * slots : (k + 1) * slots, :] = piece[slots:, :]


def source_of(count, place_ref):
    return lambda block: jnp.where(block < count, 2 * block, 2 * (block - count) + 1) ^ place_ref[0]


def least_distances(cand, points_ref, own_sq_ref):
    wide = cand.astype(jnp.float32)
    cand_sq = jnp.sum(wide * wide, axis=1, keepdims=True)
    least = None
    for start in range(0, points_ref.shape[0], 256):
        inner = lax.dot_general(
            cand, points_ref[start : start + 256, :], (((1,), (1,)), ((), ())), preferred_element_type=jnp.float32
        )
        for at in range(0, 256, LANES):
            own = own_sq_ref[:, start + at : start + at + LANES]
            dist = cand_sq + own - 2.0 * inner[:, at : at + LANES]
            least = dist if least is None else jnp.minimum(least, dist)
    return jnp.min(least, axis=1, keepdims=True)


def hold(dist_ref, before_ref, held_ref):
    def block(t, _):
        lanes = pl.ds(pl.multiple_of(t * LANES, LANES), LANES)
        before = None if before_ref is None else block16(before_ref, 0, lanes)
        for k, value in enumerate(smallest16(dist_ref, lanes, before)):
            held_ref[SUBLANES * k : SUBLANES * (k + 1), lanes] = value
        return 0

    lax.fori_loop(0, dist_ref.shape[1] // LANES, block, 0)


def even_kernel(groups, slots, cand_ref, points_ref, own_sq_ref, counts_ref, place_ref, rows_ref, held_ref, dist_ref):
    half = groups // 2 * slots
    usable = usable_slots(counts_ref, 0, half, groups, slots, source_of(groups // 2, place_ref))
    dist = distances(cand_ref[...], points_ref, own_sq_ref)
    dist_ref[...] = jnp.where(usable, dist, far_value)
    minima = jnp.where(usable, jnp.min(dist, axis=1, keepdims=True), cap_value)
    for k, row in enumerate(slot_rows(minima, slots)):
        rows_ref[k : k + 1, :] = row
    hold(dist_ref, None, held_ref)


def minima_old_kernel(groups, slots, cand_ref, points_ref, own_sq_ref, counts_ref, rows_ref, place_ref, minima_ref):
    count = groups // 2
    order = source_of(count, place_ref)
    usable = usable_slots(counts_ref, count * slots, count * slots, groups, slots, order)
    minima = jnp.where(usable, least_distances(cand_ref[...], points_ref, own_sq_ref), cap_value)
    for k, row in enumerate(slot_rows(minima, slots)):
        minima_ref[order(k)] = rows_ref[k : k + 1, :].astype(jnp.bfloat16)
        minima_ref[order(count + k)] = row.astype(jnp.bfloat16)


def odd_kernel(
    groups, slots, cand_ref, points_ref, own_sq_ref, counts_ref, place_ref, before_hbm_ref, held_ref,
    dist_ref, before_ref, sem,
):
    fetch = pltpu.make_async_copy(before_hbm_ref, before_ref, sem)
    fetch.start()
    half = groups // 2 * slots
    usable = usable_slots(counts_ref, half, half, groups, slots, source_of(groups // 2, place_ref))
    dist_ref[...] = jnp.where(usable, distances(cand_ref[...], points_ref, own_sq_ref), far_value)
    fetch.wait()
    hold(dist_ref, before_ref, held_ref)


def minima_kernel(peers, slots, cand_ref, points_ref, own_sq_ref, counts_ref, minima_ref):
    usable = usable_slots(counts_ref, 0, peers * slots, peers, slots, straight)
    minima = jnp.where(usable, least_distances(cand_ref[...], points_ref, own_sq_ref), cap_value)
    for k, row in enumerate(slot_rows(minima, slots)):
        minima_ref[k] = row.astype(jnp.bfloat16)


def select_kernel(
    peers, slots, chunk, cand_ref, points_ref, own_sq_ref, counts_ref, held_hbm_ref, out_ref, dist_ref, held_ref, sem
):
    fetch = pltpu.make_async_copy(held_hbm_ref, held_ref, sem)
    fetch.start()
    for start in range(0, peers * slots, chunk):
        usable = usable_slots(counts_ref, start, chunk, peers, slots, straight)
        dist = distances(cand_ref[start : start + chunk, :], points_ref, own_sq_ref)
        dist_ref[start : start + chunk, :] = jnp.where(usable, dist, far_value)
    fetch.wait()
    sublane = iota((SUBLANES, LANES), 0)

    def block(t, _):
        lanes = pl.ds(pl.multiple_of(t * LANES, LANES), LANES)
        held = smallest16(dist_ref, lanes, block16(held_ref, 0, lanes))
        for shift in (4, 2, 1):
            held = merge16(held, [pltpu.roll(value, shift, 0) for value in held])
        for half in range(2):
            rows = held[SUBLANES * half]
            for k in range(1, SUBLANES):
                rows = jnp.where(sublane == k, held[SUBLANES * half + k], rows)
            out_ref[SUBLANES * half : SUBLANES * (half + 1), lanes] = rows
        return 0

    lax.fori_loop(0, dist_ref.shape[1] // LANES, block, 0)


def wide_kernel(new_lists_ref, old_lists_ref, new_wide_ref, old_wide_ref):
    slots, peers = new_lists_ref.shape
    same = onehot(iota((slots, slots), 0) == iota((slots, slots), 1))

    def upright(values):
        return lax.dot_general(
            values.astype(jnp.bfloat16), same, (((0,), (0,)), ((), ())), preferred_element_type=jnp.float32
        ).astype(jnp.int32)

    new_lists = upright(new_lists_ref[...] // 32) * 32 + upright(new_lists_ref[...] % 32)
    for lists, wide_ref in ((new_lists, new_wide_ref), (old_lists_ref[...], old_wide_ref)):
        peers, slots = lists.shape
        for c in range(slots):
            wide_ref[c * peers : (c + 1) * peers, :] = jnp.broadcast_to(lists[:, c : c + 1], (peers, LANES))


def fold(best, back_ref, wide_ref):
    peers, _, slots = back_ref.shape
    total = peers * slots
    of_peer = onehot(iota((total, peers), 1) == iota((total, peers), 0) % peers)
    rows = dot(of_peer, back_ref[...].reshape(peers, slots))
    chosen = jnp.where(iota((total, slots), 1) == iota((total, slots), 0) // peers, rows, 0.0)
    values = dot(chosen.astype(jnp.bfloat16), jnp.ones((slots, LANES), jnp.bfloat16))
    lane = iota((SUBLANES, LANES), 1)
    best = list(best)
    for at in range(0, total, SUBLANES):
        index, value = wide_ref[at : at + SUBLANES, :], values[at : at + SUBLANES, :]
        for k in range(SUBLANES):
            best[k] = jnp.minimum(best[k], jnp.where(index == lane + k * LANES, value, cap_value))
    return best


def fold_new_kernel(back_ref, wide_ref, best_ref):
    best = fold([jnp.full((SUBLANES, LANES), cap_value, jnp.float32)] * SUBLANES, back_ref, wide_ref)
    for k in range(SUBLANES):
        best_ref[:, k * LANES : (k + 1) * LANES] = best[k]


def reverse_kernel(back_ref, wide_ref, best_ref, out_ref):
    best = fold([best_ref[:, k * LANES : (k + 1) * LANES] for k in range(SUBLANES)], back_ref, wide_ref)
    for k in range(SUBLANES):
        out_ref[k : k + 1, :] = jnp.min(best[k], axis=0, keepdims=True)


def apart(groups, away):
    return [(g, g ^ away) for g in range(groups)]


def body(points, serve_new, serve_old, count_new, count_old):
    rows, features = points.shape
    peers, slots = serve_new.shape
    groups, group_slots = serve_old.shape
    lists_new = serve_new.T
    counts_new, counts_old = count_new.T, count_old.T
    params = pltpu.CompilerParams(vmem_limit_bytes=VMEM_LIMIT)
    vmem = pl.BlockSpec(memory_space=pltpu.VMEM)
    smem = pl.BlockSpec(memory_space=pltpu.SMEM)
    place = lax.axis_index("grp").astype(jnp.int32).reshape(1)

    offered_new = gather_new(points, lists_new, peers, slots)
    pulled_new = lax.all_to_all(
        offered_new.reshape(peers, slots, features), "shard", split_axis=0, concat_axis=0, tiled=True
    ).reshape(peers * slots, features)

    pieces = gather_old(points, serve_old, place, groups, group_slots, groups // 2)
    spread = (4, 2, 6, 3, 7, 5, 1)
    order = tuple(k for k in spread if k < groups // 2) + tuple(range(len(spread) + 1, groups // 2))
    came = [lax.ppermute(pieces[k], "grp", apart(groups, 2 * k)) for k in order]
    own_sq = jnp.sum(jnp.square(points.astype(jnp.float32)), axis=1)[None, :]
    own_sq, own_piece = lax.optimization_barrier((own_sq, pieces[0]))

    half = groups // 2 * group_slots
    evens, handed = pl.pallas_call(
        functools.partial(halves_kernel, group_slots, order + (0,)),
        out_shape=(jax.ShapeDtypeStruct((half, features), jnp.bfloat16),) * 2,
        compiler_params=params,
        cost_estimate=pl.CostEstimate(flops=0, bytes_accessed=8 * half * features, transcendentals=0),
    )(*came, own_piece)
    odds = lax.ppermute(handed, "grp", apart(groups, 1))

    old_cost = pl.CostEstimate(
        flops=2 * half * rows * features, bytes_accessed=2 * (half + rows) * features, transcendentals=0
    )
    held_shape = (16 * SUBLANES, rows)
    minima_even, held = pl.pallas_call(
        functools.partial(even_kernel, groups, group_slots),
        in_specs=[vmem] * 4 + [smem],
        out_shape=(
            jax.ShapeDtypeStruct((groups // 2, group_slots), jnp.float32),
            pltpu.HBM(held_shape, jnp.float32),
        ),
        scratch_shapes=[pltpu.VMEM((half, rows), jnp.float32)],
        compiler_params=params,
        cost_estimate=old_cost,
    )(evens, points, own_sq, counts_old, place)
    minima_old = pl.pallas_call(
        functools.partial(minima_old_kernel, groups, group_slots),
        in_specs=[vmem] * 5 + [smem],
        out_shape=jax.ShapeDtypeStruct((groups, 1, group_slots), jnp.bfloat16),
        compiler_params=params,
        cost_estimate=old_cost,
    )(odds, points, own_sq, counts_old, minima_even, place)

    total_new = peers * slots
    minima_new = pl.pallas_call(
        functools.partial(minima_kernel, peers, slots),
        out_shape=jax.ShapeDtypeStruct((peers, 1, slots), jnp.bfloat16),
        compiler_params=params,
        cost_estimate=pl.CostEstimate(
            flops=2 * total_new * rows * features, bytes_accessed=4 * total_new * features, transcendentals=0
        ),
    )(pulled_new, points, own_sq, counts_new)

    odds, wait_lists, minima_new = lax.optimization_barrier((odds, lists_new, minima_new))
    back_new = lax.all_to_all(minima_new, "shard", split_axis=0, concat_axis=0, tiled=True)
    wide_new, wide_old = pl.pallas_call(
        wide_kernel,
        out_shape=(
            jax.ShapeDtypeStruct((total_new, LANES), jnp.int32),
            jax.ShapeDtypeStruct((groups * group_slots, LANES), jnp.int32),
        ),
        compiler_params=params,
    )(wait_lists, serve_old)
    hbm = pl.BlockSpec(memory_space=pltpu.HBM)
    held = pl.pallas_call(
        functools.partial(odd_kernel, groups, group_slots),
        in_specs=[vmem] * 4 + [smem, hbm],
        out_shape=pltpu.HBM(held_shape, jnp.float32),
        scratch_shapes=[
            pltpu.VMEM((half, rows), jnp.float32),
            pltpu.VMEM(held_shape, jnp.float32),
            pltpu.SemaphoreType.DMA,
        ],
        compiler_params=params,
        cost_estimate=old_cost,
    )(odds, points, own_sq, counts_old, place, pltpu.with_memory_space_constraint(held, pltpu.HBM))
    pulled_new, minima_old, back_new = lax.optimization_barrier((pulled_new, minima_old, back_new))
    back_old = lax.all_to_all(minima_old, "grp", split_axis=0, concat_axis=0, tiled=True)
    nearest = pl.pallas_call(
        functools.partial(select_kernel, peers, slots, 256),
        in_specs=[vmem] * 4 + [hbm],
        out_shape=jax.ShapeDtypeStruct((NEAR, rows), jnp.float32),
        scratch_shapes=[
            pltpu.VMEM((total_new, rows), jnp.float32),
            pltpu.VMEM(held_shape, jnp.float32),
            pltpu.SemaphoreType.DMA,
        ],
        compiler_params=params,
        cost_estimate=pl.CostEstimate(
            flops=4 * total_new * rows * features, bytes_accessed=4 * total_new * features, transcendentals=0
        ),
    )(pulled_new, points, own_sq, counts_new, pltpu.with_memory_space_constraint(held, pltpu.HBM))

    best = pl.pallas_call(
        fold_new_kernel,
        out_shape=jax.ShapeDtypeStruct((SUBLANES, rows), jnp.float32),
        compiler_params=params,
    )(back_new, wide_new)
    reverse = pl.pallas_call(
        reverse_kernel,
        out_shape=jax.ShapeDtypeStruct((SUBLANES, LANES), jnp.float32),
        compiler_params=params,
    )(back_old, wide_old, best)
    return nearest.T, reverse.reshape(rows)


def solution(mesh):
    placed = (P(("grp", "shard"), None),) * 5
    return jax.shard_map(
        body,
        mesh=mesh,
        in_specs=placed,
        out_specs=(P(("grp", "shard"), None), P(("grp", "shard"))),
        check_vma=False,
    )
```

```python
import functools

import jax
import jax.numpy as jnp
from jax import lax
from jax.experimental import pallas as pl
from jax.experimental.pallas import tpu as pltpu
from jax.sharding import PartitionSpec as P

NEAR = 16
LANES = 128
SUBLANES = 8

cap_value = 8.0
far_value = 1000000000.0

VMEM_LIMIT = 20 * 1024 * 1024

SORT16 = (
    (0, 13), (1, 12), (2, 15), (3, 14), (4, 8), (5, 6), (7, 11), (9, 10),
    (0, 5), (1, 7), (2, 9), (3, 4), (6, 13), (8, 14), (10, 15), (11, 12),
    (0, 1), (2, 3), (4, 5), (6, 8), (7, 9), (10, 11), (12, 13), (14, 15),
    (0, 2), (1, 3), (4, 10), (5, 11), (6, 7), (8, 9), (12, 14), (13, 15),
    (1, 2), (3, 12), (4, 6), (5, 7), (8, 10), (9, 11), (13, 14),
    (1, 4), (2, 6), (5, 8), (7, 10), (9, 13), (11, 14),
    (2, 4), (3, 6), (9, 12), (11, 13),
    (3, 5), (6, 8), (7, 9), (10, 12),
    (3, 4), (5, 6), (7, 8), (9, 10), (11, 12),
    (6, 7), (8, 9),
)


def iota(shape, dim):
    return lax.broadcasted_iota(jnp.int32, shape, dim)


def onehot(condition, dtype=jnp.bfloat16):
    return jnp.where(condition, 1.0, 0.0).astype(dtype)


def dot(a, b):
    return lax.dot_general(a, b, (((1,), (0,)), ((), ())), preferred_element_type=jnp.float32)


def flat_parts(start, count, peers, slots, order, flipped=False):
    def peer(n):
        return iota((count, n), 1) == order((iota((count, n), 0) + start) // slots)

    def slot(n):
        return iota((count, n), 1) == (iota((count, n), 0) + start) % slots

    return (slot(slots), peer(peers)) if flipped else (peer(peers), slot(slots))


def straight(block):
    return block


def index_column(lists, parts):
    rows_of, lane_of = parts
    rows_of = onehot(rows_of)
    high = dot(rows_of, (lists // 32).astype(jnp.bfloat16))
    low = dot(rows_of, (lists % 32).astype(jnp.bfloat16))
    return jnp.sum(jnp.where(lane_of, high * 32.0 + low, 0.0), axis=1, keepdims=True).astype(jnp.int32)


def gather_new_kernel(
    peers, slots, chunk, points_ref, lists_ref, out_ref, points, lists, picked, first, in_sems, out_sems
):
    total, rows = peers * slots, points_ref.shape[0]
    loads = [pltpu.make_async_copy(lists_ref, lists, in_sems.at[0])]
    for k in range(4):
        part = pl.ds(k * (rows // 4), rows // 4)
        loads.append(pltpu.make_async_copy(points_ref.at[part, :], points.at[part, :], in_sems.at[k + 1]))
    for load in loads:
        load.start()
    loads[0].wait()
    index = index_column(lists[...], flat_parts(0, total, peers, slots, straight, True))
    half = rows // 2
    stores = []
    for h in range(2):
        loads[1 + 2 * h].wait()
        loads[2 + 2 * h].wait()
        for c, at in enumerate(range(0, total, chunk)):
            picks = onehot(index[at : at + chunk, :] == iota((chunk, half), 1) + h * half)
            term = dot(picks, points[h * half : (h + 1) * half, :])
            if h == 0:
                first[at : at + chunk, :] = term
                continue
            picked[at : at + chunk, :] = (first[at : at + chunk, :] + term).astype(jnp.bfloat16)
            part = pl.ds(at, chunk)
            stores.append(pltpu.make_async_copy(picked.at[part, :], out_ref.at[part, :], out_sems.at[c]))
            stores[-1].start()
    for store in stores:
        store.wait()


def gather_new(points, lists, peers, slots):
    total, chunk = peers * slots, 128
    rows, features = points.shape
    hbm = pl.BlockSpec(memory_space=pltpu.HBM)
    return pl.pallas_call(
        functools.partial(gather_new_kernel, peers, slots, chunk),
        in_specs=[hbm, hbm],
        out_specs=hbm,
        out_shape=pltpu.HBM((total, features), jnp.bfloat16),
        scratch_shapes=[
            pltpu.VMEM((rows, features), jnp.bfloat16),
            pltpu.VMEM(lists.shape, jnp.int32),
            pltpu.VMEM((total, features), jnp.bfloat16),
            pltpu.VMEM((total, features), jnp.float32),
            pltpu.SemaphoreType.DMA((5,)),
            pltpu.SemaphoreType.DMA((total // chunk,)),
        ],
        compiler_params=pltpu.CompilerParams(vmem_limit_bytes=VMEM_LIMIT),
        cost_estimate=pl.CostEstimate(
            flops=2 * total * rows * features, bytes_accessed=2 * (total + rows) * features, transcendentals=0
        ),
    )(pltpu.with_memory_space_constraint(points, pltpu.HBM), pltpu.with_memory_space_constraint(lists, pltpu.HBM))


def gather_old_kernel(groups, slots, chunk, points_ref, lists_ref, place_ref, *outs):
    rows = points_ref.shape[0]
    size = outs[0].shape[0]
    for start in range(0, groups * slots, chunk):
        parts = flat_parts(start, chunk, groups, slots, lambda block: block ^ place_ref[0])
        index = index_column(lists_ref[...], parts)
        picked = dot(onehot(index == iota((chunk, rows), 1)), points_ref[...]).astype(jnp.bfloat16)
        for at in range(0, chunk, size):
            outs[(start + at) // size][...] = picked[at : at + size, :]


def gather_old(points, lists, place, groups, slots, pieces):
    total = groups * slots
    rows, features = points.shape
    vmem = pl.BlockSpec(memory_space=pltpu.VMEM)
    return pl.pallas_call(
        functools.partial(gather_old_kernel, groups, slots, 256),
        in_specs=[vmem, vmem, pl.BlockSpec(memory_space=pltpu.SMEM)],
        out_shape=(jax.ShapeDtypeStruct((total // pieces, features), jnp.bfloat16),) * pieces,
        compiler_params=pltpu.CompilerParams(vmem_limit_bytes=VMEM_LIMIT),
        cost_estimate=pl.CostEstimate(
            flops=2 * total * rows * features, bytes_accessed=2 * (total + rows) * features, transcendentals=0
        ),
    )(points, lists, place)


def exchange(values, low, high):
    a, b = values[low], values[high]
    values[low], values[high] = jnp.minimum(a, b), jnp.maximum(a, b)


def sort16(values):
    values = list(values)
    for low, high in SORT16:
        exchange(values, low, high)
    return values


def merge16(first, second):
    values = [jnp.minimum(first[k], second[15 - k]) for k in range(16)]
    for gap in (8, 4, 2, 1):
        for k in range(16):
            if not k & gap:
                exchange(values, k, k + gap)
    return values


def block16(ref, start, lanes):
    return [ref[pl.ds(start + SUBLANES * k, SUBLANES), lanes] for k in range(16)]


def smallest16(ref, lanes, held):
    step = 16 * SUBLANES
    first = 0
    if held is None:
        held, first = sort16(block16(ref, 0, lanes)), 1

    def body(t, held):
        start = pl.multiple_of(t * step, step)
        return tuple(merge16(held, sort16(block16(ref, start, lanes))))

    return list(lax.fori_loop(first, ref.shape[0] // step, body, tuple(held)))


def distances(cand, points_ref, own_sq_ref):
    wide = cand.astype(jnp.float32)
    cand_sq = jnp.sum(wide * wide, axis=1, keepdims=True)
    inner = lax.dot_general(
        cand, points_ref[...], (((1,), (1,)), ((), ())), preferred_element_type=jnp.float32
    )
    return cand_sq + own_sq_ref[...] - 2.0 * inner


def usable_slots(counts_ref, start, chunk, peers, slots, order):
    peer_of, _ = flat_parts(start, chunk, peers, slots, order)
    count = jnp.sum(jnp.where(peer_of, counts_ref[...], 0), axis=1, keepdims=True)
    return (iota((chunk, 1), 0) + start) % slots < count


def slot_rows(minima, slots):
    chunk = minima.shape[0]
    spread = jnp.where(iota((chunk, slots), 1) == iota((chunk, slots), 0) % slots, minima, 0.0)
    return [jnp.sum(spread[at : at + slots, :], axis=0, keepdims=True) for at in range(0, chunk, slots)]


def halves_kernel(slots, order, *refs):
    pieces, (mine_ref, handed_ref) = refs[:-2], refs[-2:]
    for k, piece in zip(order, pieces):
        mine_ref[k * slots : (k + 1) * slots, :] = piece[:slots, :]
        handed_ref[k * slots : (k + 1) * slots, :] = piece[slots:, :]


def source_of(count, place_ref):
    return lambda block: jnp.where(block < count, 2 * block, 2 * (block - count) + 1) ^ place_ref[0]


def least_distances(cand, points_ref, own_sq_ref):
    wide = cand.astype(jnp.float32)
    cand_sq = jnp.sum(wide * wide, axis=1, keepdims=True)
    least = None
    for start in range(0, points_ref.shape[0], 256):
        inner = lax.dot_general(
            cand, points_ref[start : start + 256, :], (((1,), (1,)), ((), ())), preferred_element_type=jnp.float32
        )
        for at in range(0, 256, LANES):
            own = own_sq_ref[:, start + at : start + at + LANES]
            dist = cand_sq + own - 2.0 * inner[:, at : at + LANES]
            least = dist if least is None else jnp.minimum(least, dist)
    return jnp.min(least, axis=1, keepdims=True)


def hold(dist_ref, before_ref, held_ref):
    def block(t, _):
        lanes = pl.ds(pl.multiple_of(t * LANES, LANES), LANES)
        before = None if before_ref is None else block16(before_ref, 0, lanes)
        for k, value in enumerate(smallest16(dist_ref, lanes, before)):
            held_ref[SUBLANES * k : SUBLANES * (k + 1), lanes] = value
        return 0

    lax.fori_loop(0, dist_ref.shape[1] // LANES, block, 0)


def even_kernel(groups, slots, cand_ref, points_ref, own_sq_ref, counts_ref, place_ref, rows_ref, held_ref, dist_ref):
    half = groups // 2 * slots
    usable = usable_slots(counts_ref, 0, half, groups, slots, source_of(groups // 2, place_ref))
    dist = distances(cand_ref[...], points_ref, own_sq_ref)
    dist_ref[...] = jnp.where(usable, dist, far_value)
    minima = jnp.where(usable, jnp.min(dist, axis=1, keepdims=True), cap_value)
    for k, row in enumerate(slot_rows(minima, slots)):
        rows_ref[k : k + 1, :] = row
    hold(dist_ref, None, held_ref)


def odd_kernel(
    groups, slots, cand_ref, points_ref, own_sq_ref, counts_ref, rows_ref, place_ref, before_hbm_ref,
    minima_ref, held_ref, dist_ref, before_ref, sem,
):
    fetch = pltpu.make_async_copy(before_hbm_ref, before_ref, sem)
    fetch.start()
    count = groups // 2
    order = source_of(count, place_ref)
    usable = usable_slots(counts_ref, count * slots, count * slots, groups, slots, order)
    dist = distances(cand_ref[...], points_ref, own_sq_ref)
    dist_ref[...] = jnp.where(usable, dist, far_value)
    minima = jnp.where(usable, jnp.min(dist, axis=1, keepdims=True), cap_value)
    for k, row in enumerate(slot_rows(minima, slots)):
        minima_ref[order(k)] = rows_ref[k : k + 1, :].astype(jnp.bfloat16)
        minima_ref[order(count + k)] = row.astype(jnp.bfloat16)
    fetch.wait()
    hold(dist_ref, before_ref, held_ref)


def minima_kernel(peers, slots, cand_ref, points_ref, own_sq_ref, counts_ref, minima_ref):
    usable = usable_slots(counts_ref, 0, peers * slots, peers, slots, straight)
    minima = jnp.where(usable, least_distances(cand_ref[...], points_ref, own_sq_ref), cap_value)
    for k, row in enumerate(slot_rows(minima, slots)):
        minima_ref[k] = row.astype(jnp.bfloat16)


def select_kernel(
    peers, slots, chunk, cand_ref, points_ref, own_sq_ref, counts_ref, held_hbm_ref, out_ref, dist_ref, held_ref, sem
):
    fetch = pltpu.make_async_copy(held_hbm_ref, held_ref, sem)
    fetch.start()
    for start in range(0, peers * slots, chunk):
        usable = usable_slots(counts_ref, start, chunk, peers, slots, straight)
        dist = distances(cand_ref[start : start + chunk, :], points_ref, own_sq_ref)
        dist_ref[start : start + chunk, :] = jnp.where(usable, dist, far_value)
    fetch.wait()
    sublane = iota((SUBLANES, LANES), 0)

    def block(t, _):
        lanes = pl.ds(pl.multiple_of(t * LANES, LANES), LANES)
        held = smallest16(dist_ref, lanes, block16(held_ref, 0, lanes))
        for shift in (4, 2, 1):
            held = merge16(held, [pltpu.roll(value, shift, 0) for value in held])
        for half in range(2):
            rows = held[SUBLANES * half]
            for k in range(1, SUBLANES):
                rows = jnp.where(sublane == k, held[SUBLANES * half + k], rows)
            out_ref[SUBLANES * half : SUBLANES * (half + 1), lanes] = rows
        return 0

    lax.fori_loop(0, dist_ref.shape[1] // LANES, block, 0)


def ready_kernel(old_lists_ref, old_back_ref, new_lists_ref, best_ref, wide_ref):
    best = jnp.full(best_ref.shape, cap_value, jnp.float32)
    old_back = old_back_ref[...].reshape(old_lists_ref.shape).astype(jnp.float32)
    peers, slots = old_lists_ref.shape
    for c in range(slots):
        for at in range(0, peers, SUBLANES):
            index = old_lists_ref[at : at + SUBLANES, c : c + 1]
            value = old_back[at : at + SUBLANES, c : c + 1]
            best = jnp.where(index == iota(best.shape, 1), jnp.minimum(best, value), best)
    best_ref[...] = best
    slots, peers = new_lists_ref.shape
    same = onehot(iota((slots, slots), 0) == iota((slots, slots), 1))

    def upright(values):
        return lax.dot_general(
            values.astype(jnp.bfloat16), same, (((0,), (0,)), ((), ())), preferred_element_type=jnp.float32
        ).astype(jnp.int32)

    lists = upright(new_lists_ref[...] // 32) * 32 + upright(new_lists_ref[...] % 32)
    for c in range(slots):
        wide_ref[c * peers : (c + 1) * peers, :] = jnp.broadcast_to(lists[:, c : c + 1], (peers, LANES))


def reverse_kernel(back_ref, best_ref, wide_ref, out_ref):
    peers, _, slots = back_ref.shape
    total = peers * slots
    of_peer = onehot(iota((total, peers), 1) == iota((total, peers), 0) % peers)
    rows = dot(of_peer, back_ref[...].reshape(peers, slots))
    chosen = jnp.where(iota((total, slots), 1) == iota((total, slots), 0) // peers, rows, 0.0)
    values = dot(chosen.astype(jnp.bfloat16), jnp.ones((slots, LANES), jnp.bfloat16))
    lane = iota((SUBLANES, LANES), 1)
    best = [best_ref[:, LANES * k : LANES * (k + 1)] for k in range(SUBLANES)]
    for at in range(0, total, SUBLANES):
        index, value = wide_ref[at : at + SUBLANES, :], values[at : at + SUBLANES, :]
        for k in range(SUBLANES):
            best[k] = jnp.minimum(best[k], jnp.where(index == lane + k * LANES, value, cap_value))
    for k in range(SUBLANES):
        out_ref[k : k + 1, :] = jnp.min(best[k], axis=0, keepdims=True)


def apart(groups, away):
    return [(g, g ^ away) for g in range(groups)]


def body(points, serve_new, serve_old, count_new, count_old):
    rows, features = points.shape
    peers, slots = serve_new.shape
    groups, group_slots = serve_old.shape
    lists_new = serve_new.T
    counts_new, counts_old = count_new.T, count_old.T
    params = pltpu.CompilerParams(vmem_limit_bytes=VMEM_LIMIT)
    vmem = pl.BlockSpec(memory_space=pltpu.VMEM)
    smem = pl.BlockSpec(memory_space=pltpu.SMEM)
    place = lax.axis_index("grp").astype(jnp.int32).reshape(1)

    offered_new = gather_new(points, lists_new, peers, slots)
    pulled_new = lax.all_to_all(
        offered_new.reshape(peers, slots, features), "shard", split_axis=0, concat_axis=0, tiled=True
    ).reshape(peers * slots, features)

    pieces = gather_old(points, serve_old, place, groups, group_slots, groups // 2)
    spread = (4, 2, 6, 3, 7, 5, 1)
    order = tuple(k for k in spread if k < groups // 2) + tuple(range(len(spread) + 1, groups // 2))
    came = [lax.ppermute(pieces[k], "grp", apart(groups, 2 * k)) for k in order]
    own_sq = jnp.sum(jnp.square(points.astype(jnp.float32)), axis=1)[None, :]
    own_sq, own_piece = lax.optimization_barrier((own_sq, pieces[0]))

    half = groups // 2 * group_slots
    evens, handed = pl.pallas_call(
        functools.partial(halves_kernel, group_slots, order + (0,)),
        out_shape=(jax.ShapeDtypeStruct((half, features), jnp.bfloat16),) * 2,
        compiler_params=params,
        cost_estimate=pl.CostEstimate(flops=0, bytes_accessed=8 * half * features, transcendentals=0),
    )(*came, own_piece)
    odds = lax.ppermute(handed, "grp", apart(groups, 1))

    old_cost = pl.CostEstimate(
        flops=2 * half * rows * features, bytes_accessed=2 * (half + rows) * features, transcendentals=0
    )
    held_shape = (16 * SUBLANES, rows)
    minima_even, held = pl.pallas_call(
        functools.partial(even_kernel, groups, group_slots),
        in_specs=[vmem] * 4 + [smem],
        out_shape=(
            jax.ShapeDtypeStruct((groups // 2, group_slots), jnp.float32),
            pltpu.HBM(held_shape, jnp.float32),
        ),
        scratch_shapes=[pltpu.VMEM((half, rows), jnp.float32)],
        compiler_params=params,
        cost_estimate=old_cost,
    )(evens, points, own_sq, counts_old, place)
    hbm = pl.BlockSpec(memory_space=pltpu.HBM)
    minima_old, held = pl.pallas_call(
        functools.partial(odd_kernel, groups, group_slots),
        in_specs=[vmem] * 5 + [smem, hbm],
        out_shape=(
            jax.ShapeDtypeStruct((groups, 1, group_slots), jnp.bfloat16),
            pltpu.HBM(held_shape, jnp.float32),
        ),
        scratch_shapes=[
            pltpu.VMEM((half, rows), jnp.float32),
            pltpu.VMEM(held_shape, jnp.float32),
            pltpu.SemaphoreType.DMA,
        ],
        compiler_params=params,
        cost_estimate=old_cost,
    )(odds, points, own_sq, counts_old, minima_even, place, pltpu.with_memory_space_constraint(held, pltpu.HBM))

    pulled_new, minima_old = lax.optimization_barrier((pulled_new, minima_old))
    back_old = lax.all_to_all(minima_old, "grp", split_axis=0, concat_axis=0, tiled=True)

    total_new = peers * slots
    minima_new = pl.pallas_call(
        functools.partial(minima_kernel, peers, slots),
        out_shape=jax.ShapeDtypeStruct((peers, 1, slots), jnp.bfloat16),
        compiler_params=params,
        cost_estimate=pl.CostEstimate(
            flops=2 * total_new * rows * features, bytes_accessed=4 * total_new * features, transcendentals=0
        ),
    )(pulled_new, points, own_sq, counts_new)
    back_new = lax.all_to_all(minima_new, "shard", split_axis=0, concat_axis=0, tiled=True)

    pulled_new, back_old, _ = lax.optimization_barrier((pulled_new, back_old, minima_new))
    nearest = pl.pallas_call(
        functools.partial(select_kernel, peers, slots, 256),
        in_specs=[vmem] * 4 + [hbm],
        out_shape=jax.ShapeDtypeStruct((NEAR, rows), jnp.float32),
        scratch_shapes=[
            pltpu.VMEM((total_new, rows), jnp.float32),
            pltpu.VMEM(held_shape, jnp.float32),
            pltpu.SemaphoreType.DMA,
        ],
        compiler_params=params,
        cost_estimate=pl.CostEstimate(
            flops=4 * total_new * rows * features, bytes_accessed=4 * total_new * features, transcendentals=0
        ),
    )(pulled_new, points, own_sq, counts_new, pltpu.with_memory_space_constraint(held, pltpu.HBM))

    nearest, back_old = lax.optimization_barrier((nearest, back_old))
    best, wide = pl.pallas_call(
        ready_kernel,
        out_shape=(
            jax.ShapeDtypeStruct((SUBLANES, rows), jnp.float32),
            jax.ShapeDtypeStruct((total_new, LANES), jnp.int32),
        ),
        compiler_params=params,
    )(serve_old, back_old, lists_new)
    reverse = pl.pallas_call(
        reverse_kernel,
        out_shape=jax.ShapeDtypeStruct((SUBLANES, LANES), jnp.float32),
        compiler_params=params,
    )(back_new, best, wide)
    return nearest.T, reverse.reshape(rows)


def solution(mesh):
    placed = (P(("grp", "shard"), None),) * 5
    return jax.shard_map(
        body,
        mesh=mesh,
        in_specs=placed,
        out_specs=(P(("grp", "shard"), None), P(("grp", "shard"))),
        check_vma=False,
    )
```

```python
import functools

import jax
import jax.numpy as jnp
from jax import lax
from jax.experimental import pallas as pl
from jax.experimental.pallas import tpu as pltpu
from jax.sharding import PartitionSpec as P

NEAR = 16
LANES = 128
SUBLANES = 8

cap_value = 8.0
far_value = 1000000000.0

VMEM_LIMIT = 20 * 1024 * 1024

SORT16 = (
    (0, 13), (1, 12), (2, 15), (3, 14), (4, 8), (5, 6), (7, 11), (9, 10),
    (0, 5), (1, 7), (2, 9), (3, 4), (6, 13), (8, 14), (10, 15), (11, 12),
    (0, 1), (2, 3), (4, 5), (6, 8), (7, 9), (10, 11), (12, 13), (14, 15),
    (0, 2), (1, 3), (4, 10), (5, 11), (6, 7), (8, 9), (12, 14), (13, 15),
    (1, 2), (3, 12), (4, 6), (5, 7), (8, 10), (9, 11), (13, 14),
    (1, 4), (2, 6), (5, 8), (7, 10), (9, 13), (11, 14),
    (2, 4), (3, 6), (9, 12), (11, 13),
    (3, 5), (6, 8), (7, 9), (10, 12),
    (3, 4), (5, 6), (7, 8), (9, 10), (11, 12),
    (6, 7), (8, 9),
)


def iota(shape, dim):
    return lax.broadcasted_iota(jnp.int32, shape, dim)


def onehot(condition, dtype=jnp.bfloat16):
    return jnp.where(condition, 1.0, 0.0).astype(dtype)


def dot(a, b):
    return lax.dot_general(a, b, (((1,), (0,)), ((), ())), preferred_element_type=jnp.float32)


def flat_parts(start, count, peers, slots, order, flipped=False):
    def peer(n):
        return iota((count, n), 1) == order((iota((count, n), 0) + start) // slots)

    def slot(n):
        return iota((count, n), 1) == (iota((count, n), 0) + start) % slots

    return (slot(slots), peer(peers)) if flipped else (peer(peers), slot(slots))


def straight(block):
    return block


def index_column(lists, parts):
    rows_of, lane_of = parts
    rows_of = onehot(rows_of)
    high = dot(rows_of, (lists // 32).astype(jnp.bfloat16))
    low = dot(rows_of, (lists % 32).astype(jnp.bfloat16))
    return jnp.sum(jnp.where(lane_of, high * 32.0 + low, 0.0), axis=1, keepdims=True).astype(jnp.int32)


def gather_new_kernel(
    peers, slots, chunk, points_ref, lists_ref, out_ref, points, lists, picked, first, in_sems, out_sems
):
    total, rows = peers * slots, points_ref.shape[0]
    loads = [pltpu.make_async_copy(lists_ref, lists, in_sems.at[0])]
    for k in range(4):
        part = pl.ds(k * (rows // 4), rows // 4)
        loads.append(pltpu.make_async_copy(points_ref.at[part, :], points.at[part, :], in_sems.at[k + 1]))
    for load in loads:
        load.start()
    loads[0].wait()
    index = index_column(lists[...], flat_parts(0, total, peers, slots, straight, True))
    half = rows // 2
    stores = []
    for h in range(2):
        loads[1 + 2 * h].wait()
        loads[2 + 2 * h].wait()
        for c, at in enumerate(range(0, total, chunk)):
            picks = onehot(index[at : at + chunk, :] == iota((chunk, half), 1) + h * half)
            term = dot(picks, points[h * half : (h + 1) * half, :])
            if h == 0:
                first[at : at + chunk, :] = term
                continue
            picked[at : at + chunk, :] = (first[at : at + chunk, :] + term).astype(jnp.bfloat16)
            part = pl.ds(at, chunk)
            stores.append(pltpu.make_async_copy(picked.at[part, :], out_ref.at[part, :], out_sems.at[c]))
            stores[-1].start()
    for store in stores:
        store.wait()


def gather_new(points, lists, peers, slots):
    total, chunk = peers * slots, 128
    rows, features = points.shape
    hbm = pl.BlockSpec(memory_space=pltpu.HBM)
    return pl.pallas_call(
        functools.partial(gather_new_kernel, peers, slots, chunk),
        in_specs=[hbm, hbm],
        out_specs=hbm,
        out_shape=pltpu.HBM((total, features), jnp.bfloat16),
        scratch_shapes=[
            pltpu.VMEM((rows, features), jnp.bfloat16),
            pltpu.VMEM(lists.shape, jnp.int32),
            pltpu.VMEM((total, features), jnp.bfloat16),
            pltpu.VMEM((total, features), jnp.float32),
            pltpu.SemaphoreType.DMA((5,)),
            pltpu.SemaphoreType.DMA((total // chunk,)),
        ],
        compiler_params=pltpu.CompilerParams(vmem_limit_bytes=VMEM_LIMIT),
        cost_estimate=pl.CostEstimate(
            flops=2 * total * rows * features, bytes_accessed=2 * (total + rows) * features, transcendentals=0
        ),
    )(pltpu.with_memory_space_constraint(points, pltpu.HBM), pltpu.with_memory_space_constraint(lists, pltpu.HBM))


def gather_old_kernel(groups, slots, chunk, points_ref, lists_ref, place_ref, *outs):
    rows = points_ref.shape[0]
    size = outs[0].shape[0]
    for start in range(0, groups * slots, chunk):
        parts = flat_parts(start, chunk, groups, slots, lambda block: block ^ place_ref[0])
        index = index_column(lists_ref[...], parts)
        picked = dot(onehot(index == iota((chunk, rows), 1)), points_ref[...]).astype(jnp.bfloat16)
        for at in range(0, chunk, size):
            outs[(start + at) // size][...] = picked[at : at + size, :]


def gather_old(points, lists, place, groups, slots, pieces):
    total = groups * slots
    rows, features = points.shape
    vmem = pl.BlockSpec(memory_space=pltpu.VMEM)
    return pl.pallas_call(
        functools.partial(gather_old_kernel, groups, slots, 256),
        in_specs=[vmem, vmem, pl.BlockSpec(memory_space=pltpu.SMEM)],
        out_shape=(jax.ShapeDtypeStruct((total // pieces, features), jnp.bfloat16),) * pieces,
        compiler_params=pltpu.CompilerParams(vmem_limit_bytes=VMEM_LIMIT),
        cost_estimate=pl.CostEstimate(
            flops=2 * total * rows * features, bytes_accessed=2 * (total + rows) * features, transcendentals=0
        ),
    )(points, lists, place)


def exchange(values, low, high):
    a, b = values[low], values[high]
    values[low], values[high] = jnp.minimum(a, b), jnp.maximum(a, b)


def sort16(values):
    values = list(values)
    for low, high in SORT16:
        exchange(values, low, high)
    return values


def merge16(first, second):
    values = [jnp.minimum(first[k], second[15 - k]) for k in range(16)]
    for gap in (8, 4, 2, 1):
        for k in range(16):
            if not k & gap:
                exchange(values, k, k + gap)
    return values


def block16(ref, start, lanes):
    return [ref[pl.ds(start + SUBLANES * k, SUBLANES), lanes] for k in range(16)]


def smallest16(ref, lanes, held):
    step = 16 * SUBLANES
    first = 0
    if held is None:
        held, first = sort16(block16(ref, 0, lanes)), 1

    def body(t, held):
        start = pl.multiple_of(t * step, step)
        return tuple(merge16(held, sort16(block16(ref, start, lanes))))

    return list(lax.fori_loop(first, ref.shape[0] // step, body, tuple(held)))


def distances(cand, points_ref, own_sq_ref):
    wide = cand.astype(jnp.float32)
    cand_sq = jnp.sum(wide * wide, axis=1, keepdims=True)
    inner = lax.dot_general(
        cand, points_ref[...], (((1,), (1,)), ((), ())), preferred_element_type=jnp.float32
    )
    return cand_sq + own_sq_ref[...] - 2.0 * inner


def usable_slots(counts_ref, start, chunk, peers, slots, order):
    peer_of, _ = flat_parts(start, chunk, peers, slots, order)
    count = jnp.sum(jnp.where(peer_of, counts_ref[...], 0), axis=1, keepdims=True)
    return (iota((chunk, 1), 0) + start) % slots < count


def slot_rows(minima, slots):
    chunk = minima.shape[0]
    spread = jnp.where(iota((chunk, slots), 1) == iota((chunk, slots), 0) % slots, minima, 0.0)
    return [jnp.sum(spread[at : at + slots, :], axis=0, keepdims=True) for at in range(0, chunk, slots)]


def halves_kernel(slots, order, *refs):
    pieces, (mine_ref, handed_ref) = refs[:-2], refs[-2:]
    for k, piece in zip(order, pieces):
        mine_ref[k * slots : (k + 1) * slots, :] = piece[:slots, :]
        handed_ref[k * slots : (k + 1) * slots, :] = piece[slots:, :]


def source_of(count, place_ref):
    return lambda block: jnp.where(block < count, 2 * block, 2 * (block - count) + 1) ^ place_ref[0]


def least_distances(cand, points_ref, own_sq_ref):
    wide = cand.astype(jnp.float32)
    cand_sq = jnp.sum(wide * wide, axis=1, keepdims=True)
    least = None
    for start in range(0, points_ref.shape[0], 256):
        inner = lax.dot_general(
            cand, points_ref[start : start + 256, :], (((1,), (1,)), ((), ())), preferred_element_type=jnp.float32
        )
        for at in range(0, 256, LANES):
            own = own_sq_ref[:, start + at : start + at + LANES]
            dist = cand_sq + own - 2.0 * inner[:, at : at + LANES]
            least = dist if least is None else jnp.minimum(least, dist)
    return jnp.min(least, axis=1, keepdims=True)


def hold(dist_ref, before_ref, held_ref):
    def block(t, _):
        lanes = pl.ds(pl.multiple_of(t * LANES, LANES), LANES)
        before = None if before_ref is None else block16(before_ref, 0, lanes)
        for k, value in enumerate(smallest16(dist_ref, lanes, before)):
            held_ref[SUBLANES * k : SUBLANES * (k + 1), lanes] = value
        return 0

    lax.fori_loop(0, dist_ref.shape[1] // LANES, block, 0)


def even_kernel(groups, slots, cand_ref, points_ref, own_sq_ref, counts_ref, place_ref, rows_ref, held_ref, dist_ref):
    half = groups // 2 * slots
    usable = usable_slots(counts_ref, 0, half, groups, slots, source_of(groups // 2, place_ref))
    dist = distances(cand_ref[...], points_ref, own_sq_ref)
    dist_ref[...] = jnp.where(usable, dist, far_value)
    minima = jnp.where(usable, jnp.min(dist, axis=1, keepdims=True), cap_value)
    for k, row in enumerate(slot_rows(minima, slots)):
        rows_ref[k : k + 1, :] = row
    hold(dist_ref, None, held_ref)


def minima_old_kernel(groups, slots, cand_ref, points_ref, own_sq_ref, counts_ref, rows_ref, place_ref, minima_ref):
    count = groups // 2
    order = source_of(count, place_ref)
    usable = usable_slots(counts_ref, count * slots, count * slots, groups, slots, order)
    minima = jnp.where(usable, least_distances(cand_ref[...], points_ref, own_sq_ref), cap_value)
    for k, row in enumerate(slot_rows(minima, slots)):
        minima_ref[order(k)] = rows_ref[k : k + 1, :].astype(jnp.bfloat16)
        minima_ref[order(count + k)] = row.astype(jnp.bfloat16)


def odd_kernel(
    groups, slots, cand_ref, points_ref, own_sq_ref, counts_ref, place_ref, before_hbm_ref, held_ref,
    dist_ref, before_ref, sem,
):
    fetch = pltpu.make_async_copy(before_hbm_ref, before_ref, sem)
    fetch.start()
    half = groups // 2 * slots
    usable = usable_slots(counts_ref, half, half, groups, slots, source_of(groups // 2, place_ref))
    dist_ref[...] = jnp.where(usable, distances(cand_ref[...], points_ref, own_sq_ref), far_value)
    fetch.wait()
    hold(dist_ref, before_ref, held_ref)


def minima_kernel(peers, slots, cand_ref, points_ref, own_sq_ref, counts_ref, minima_ref):
    usable = usable_slots(counts_ref, 0, peers * slots, peers, slots, straight)
    minima = jnp.where(usable, least_distances(cand_ref[...], points_ref, own_sq_ref), cap_value)
    for k, row in enumerate(slot_rows(minima, slots)):
        minima_ref[k] = row.astype(jnp.bfloat16)


def select_kernel(
    peers, slots, chunk, cand_ref, points_ref, own_sq_ref, counts_ref, held_hbm_ref, out_ref, dist_ref, held_ref, sem
):
    fetch = pltpu.make_async_copy(held_hbm_ref, held_ref, sem)
    fetch.start()
    for start in range(0, peers * slots, chunk):
        usable = usable_slots(counts_ref, start, chunk, peers, slots, straight)
        dist = distances(cand_ref[start : start + chunk, :], points_ref, own_sq_ref)
        dist_ref[start : start + chunk, :] = jnp.where(usable, dist, far_value)
    fetch.wait()
    sublane = iota((SUBLANES, LANES), 0)

    def block(t, _):
        lanes = pl.ds(pl.multiple_of(t * LANES, LANES), LANES)
        held = smallest16(dist_ref, lanes, block16(held_ref, 0, lanes))
        for shift in (4, 2, 1):
            held = merge16(held, [pltpu.roll(value, shift, 0) for value in held])
        for half in range(2):
            rows = held[SUBLANES * half]
            for k in range(1, SUBLANES):
                rows = jnp.where(sublane == k, held[SUBLANES * half + k], rows)
            out_ref[SUBLANES * half : SUBLANES * (half + 1), lanes] = rows
        return 0

    lax.fori_loop(0, dist_ref.shape[1] // LANES, block, 0)


def ready_kernel(old_lists_ref, old_back_ref, new_lists_ref, best_ref, wide_ref):
    best = jnp.full(best_ref.shape, cap_value, jnp.float32)
    old_back = old_back_ref[...].reshape(old_lists_ref.shape).astype(jnp.float32)
    peers, slots = old_lists_ref.shape
    for c in range(slots):
        for at in range(0, peers, SUBLANES):
            index = old_lists_ref[at : at + SUBLANES, c : c + 1]
            value = old_back[at : at + SUBLANES, c : c + 1]
            best = jnp.where(index == iota(best.shape, 1), jnp.minimum(best, value), best)
    best_ref[...] = best
    slots, peers = new_lists_ref.shape
    same = onehot(iota((slots, slots), 0) == iota((slots, slots), 1))

    def upright(values):
        return lax.dot_general(
            values.astype(jnp.bfloat16), same, (((0,), (0,)), ((), ())), preferred_element_type=jnp.float32
        ).astype(jnp.int32)

    lists = upright(new_lists_ref[...] // 32) * 32 + upright(new_lists_ref[...] % 32)
    for c in range(slots):
        wide_ref[c * peers : (c + 1) * peers, :] = jnp.broadcast_to(lists[:, c : c + 1], (peers, LANES))


def reverse_kernel(back_ref, best_ref, wide_ref, out_ref):
    peers, _, slots = back_ref.shape
    total = peers * slots
    of_peer = onehot(iota((total, peers), 1) == iota((total, peers), 0) % peers)
    rows = dot(of_peer, back_ref[...].reshape(peers, slots))
    chosen = jnp.where(iota((total, slots), 1) == iota((total, slots), 0) // peers, rows, 0.0)
    values = dot(chosen.astype(jnp.bfloat16), jnp.ones((slots, LANES), jnp.bfloat16))
    lane = iota((SUBLANES, LANES), 1)
    best = [best_ref[:, LANES * k : LANES * (k + 1)] for k in range(SUBLANES)]
    for at in range(0, total, SUBLANES):
        index, value = wide_ref[at : at + SUBLANES, :], values[at : at + SUBLANES, :]
        for k in range(SUBLANES):
            best[k] = jnp.minimum(best[k], jnp.where(index == lane + k * LANES, value, cap_value))
    for k in range(SUBLANES):
        out_ref[k : k + 1, :] = jnp.min(best[k], axis=0, keepdims=True)


def apart(groups, away):
    return [(g, g ^ away) for g in range(groups)]


def body(points, serve_new, serve_old, count_new, count_old):
    rows, features = points.shape
    peers, slots = serve_new.shape
    groups, group_slots = serve_old.shape
    lists_new = serve_new.T
    counts_new, counts_old = count_new.T, count_old.T
    params = pltpu.CompilerParams(vmem_limit_bytes=VMEM_LIMIT)
    vmem = pl.BlockSpec(memory_space=pltpu.VMEM)
    smem = pl.BlockSpec(memory_space=pltpu.SMEM)
    place = lax.axis_index("grp").astype(jnp.int32).reshape(1)

    offered_new = gather_new(points, lists_new, peers, slots)
    pulled_new = lax.all_to_all(
        offered_new.reshape(peers, slots, features), "shard", split_axis=0, concat_axis=0, tiled=True
    ).reshape(peers * slots, features)

    pieces = gather_old(points, serve_old, place, groups, group_slots, groups // 2)
    spread = (4, 2, 6, 3, 7, 5, 1)
    order = tuple(k for k in spread if k < groups // 2) + tuple(range(len(spread) + 1, groups // 2))
    came = [lax.ppermute(pieces[k], "grp", apart(groups, 2 * k)) for k in order]
    own_sq = jnp.sum(jnp.square(points.astype(jnp.float32)), axis=1)[None, :]
    own_sq, own_piece = lax.optimization_barrier((own_sq, pieces[0]))

    half = groups // 2 * group_slots
    evens, handed = pl.pallas_call(
        functools.partial(halves_kernel, group_slots, order + (0,)),
        out_shape=(jax.ShapeDtypeStruct((half, features), jnp.bfloat16),) * 2,
        compiler_params=params,
        cost_estimate=pl.CostEstimate(flops=0, bytes_accessed=8 * half * features, transcendentals=0),
    )(*came, own_piece)
    odds = lax.ppermute(handed, "grp", apart(groups, 1))

    old_cost = pl.CostEstimate(
        flops=2 * half * rows * features, bytes_accessed=2 * (half + rows) * features, transcendentals=0
    )
    held_shape = (16 * SUBLANES, rows)
    minima_even, held = pl.pallas_call(
        functools.partial(even_kernel, groups, group_slots),
        in_specs=[vmem] * 4 + [smem],
        out_shape=(
            jax.ShapeDtypeStruct((groups // 2, group_slots), jnp.float32),
            pltpu.HBM(held_shape, jnp.float32),
        ),
        scratch_shapes=[pltpu.VMEM((half, rows), jnp.float32)],
        compiler_params=params,
        cost_estimate=old_cost,
    )(evens, points, own_sq, counts_old, place)
    minima_old = pl.pallas_call(
        functools.partial(minima_old_kernel, groups, group_slots),
        in_specs=[vmem] * 5 + [smem],
        out_shape=jax.ShapeDtypeStruct((groups, 1, group_slots), jnp.bfloat16),
        compiler_params=params,
        cost_estimate=old_cost,
    )(odds, points, own_sq, counts_old, minima_even, place)

    pulled_new, minima_old = lax.optimization_barrier((pulled_new, minima_old))
    back_old = lax.all_to_all(minima_old, "grp", split_axis=0, concat_axis=0, tiled=True)

    total_new = peers * slots
    minima_new = pl.pallas_call(
        functools.partial(minima_kernel, peers, slots),
        out_shape=jax.ShapeDtypeStruct((peers, 1, slots), jnp.bfloat16),
        compiler_params=params,
        cost_estimate=pl.CostEstimate(
            flops=2 * total_new * rows * features, bytes_accessed=4 * total_new * features, transcendentals=0
        ),
    )(pulled_new, points, own_sq, counts_new)
    back_new = lax.all_to_all(minima_new, "shard", split_axis=0, concat_axis=0, tiled=True)

    odds, _ = lax.optimization_barrier((odds, pulled_new))
    hbm = pl.BlockSpec(memory_space=pltpu.HBM)
    held = pl.pallas_call(
        functools.partial(odd_kernel, groups, group_slots),
        in_specs=[vmem] * 4 + [smem, hbm],
        out_shape=pltpu.HBM(held_shape, jnp.float32),
        scratch_shapes=[
            pltpu.VMEM((half, rows), jnp.float32),
            pltpu.VMEM(held_shape, jnp.float32),
            pltpu.SemaphoreType.DMA,
        ],
        compiler_params=params,
        cost_estimate=old_cost,
    )(odds, points, own_sq, counts_old, place, pltpu.with_memory_space_constraint(held, pltpu.HBM))
    pulled_new, back_old, _ = lax.optimization_barrier((pulled_new, back_old, minima_new))
    nearest = pl.pallas_call(
        functools.partial(select_kernel, peers, slots, 256),
        in_specs=[vmem] * 4 + [hbm],
        out_shape=jax.ShapeDtypeStruct((NEAR, rows), jnp.float32),
        scratch_shapes=[
            pltpu.VMEM((total_new, rows), jnp.float32),
            pltpu.VMEM(held_shape, jnp.float32),
            pltpu.SemaphoreType.DMA,
        ],
        compiler_params=params,
        cost_estimate=pl.CostEstimate(
            flops=4 * total_new * rows * features, bytes_accessed=4 * total_new * features, transcendentals=0
        ),
    )(pulled_new, points, own_sq, counts_new, pltpu.with_memory_space_constraint(held, pltpu.HBM))

    nearest, back_old = lax.optimization_barrier((nearest, back_old))
    best, wide = pl.pallas_call(
        ready_kernel,
        out_shape=(
            jax.ShapeDtypeStruct((SUBLANES, rows), jnp.float32),
            jax.ShapeDtypeStruct((total_new, LANES), jnp.int32),
        ),
        compiler_params=params,
    )(serve_old, back_old, lists_new)
    reverse = pl.pallas_call(
        reverse_kernel,
        out_shape=jax.ShapeDtypeStruct((SUBLANES, LANES), jnp.float32),
        compiler_params=params,
    )(back_new, best, wide)
    return nearest.T, reverse.reshape(rows)


def solution(mesh):
    placed = (P(("grp", "shard"), None),) * 5
    return jax.shard_map(
        body,
        mesh=mesh,
        in_specs=placed,
        out_specs=(P(("grp", "shard"), None), P(("grp", "shard"))),
        check_vma=False,
    )
```
